512 devices in a mesh: pipe: 16 (over y, z_lo), expert: 32 (over x, z_hi, core).
Axes of the slice: x: 4, y: 4, z: 16 (z_hi: 4, z_lo: 4; z = z_hi * 4 + z_lo), core: 2. Of those that a mesh axis runs over, the one named last changes fastest.
Arguments:
- forward_input: bfloat16 [16, 512, 3584], P('pipe', 'expert'), may hold values from -6 to 6
- backward_input: bfloat16 [16, 512, 3584], P('pipe', 'expert'), may hold values from -6 to 6
- backward_grad: bfloat16 [16, 512, 3584], P('pipe', 'expert'), may hold values from -6 to 6
- gate_up_weight: bfloat16 [16, 3584, 8192], P('pipe', None, 'expert'), may hold values from -0.09375 to 0.09375
- down_weight: bfloat16 [16, 4096, 3584], P('pipe', 'expert'), may hold values from -0.1875 to 0.1875
- forward_routes: int32 [16, 512, 2], P('pipe', 'expert'), may hold values from 0 to 3, all different within a row; in each aligned block of 16 rows (0 to 15, 16 to 31, ..., all dimensions but the last counted through in order) at most 12 rows name the same one
- backward_routes: int32 [16, 512, 2], P('pipe', 'expert'), may hold values from 0 to 3, all different within a row; in each aligned block of 16 rows (0 to 15, 16 to 31, ..., all dimensions but the last counted through in order) at most 12 rows name the same one
- forward_gates: float32 [16, 512, 2], P('pipe', 'expert'), may hold values from 0.1 to 1
- backward_gates: float32 [16, 512, 2], P('pipe', 'expert'), may hold values from 0.1 to 1
Outputs:
- forward_next: bfloat16 [16, 512, 3584], P('pipe', 'expert')
- backward_next: bfloat16 [16, 512, 3584], P('pipe', 'expert')
The draws below stay inside these ranges and needn't reach their ends.
Inputs may be any that keep to these rules, and one draw needn't show every extreme that they name: `forward_routes`: A token names 2 different experts. Within the 16 tokens of one device at one section no expert is named more than 12 times, and in some such blocks one expert is named exactly 12 times. `backward_routes`: as for forward_routes.
All inputs are finite; a program needn't handle non-finite values.
Results may differ from the reference program's by a relative error of at most 0.0041.
Values may be sent and summed in bfloat16 or wider, within the bound.
No kernel may reach another device: no remote copies, remote signals or barrier semaphores. Data moves between devices by JAX's collectives and lax.ppermute only.
A program may use at most 128 MiB of HBM per device.

```python
import math
import jax
import jax.numpy as jnp
import numpy as np
from jax import lax

D = 3584
HID = 1024
EXPERTS = 4
TOPK = 2
TOK_DEV = 16
CAP = 12
TOKENS = 512
SECTIONS = 16
N_EXPERT = 32


def block_scale(rng, shape, split, smallest, top_value):
    def one(axis_at, parts):
        steps = jax.random.uniform(jax.random.fold_in(jax.random.fold_in(rng, 6), axis_at), (parts,), jnp.float32, smallest / len(split), top_value / len(split))
        return jnp.repeat(jnp.exp(steps), shape[axis_at] // parts).reshape((-1,) + (1,) * (len(shape) - axis_at - 1))

    level = one(*split[0])
    for cut in split[1:]:
        level = level * one(*cut)
    return level


def deal_out(own_key, own, number, rows, number_of, top, reach, lean):
    sequence = jax.random.permutation(own_key, number_of)
    heavy_load, common = load_shares(number_of, rows * top, reach, lean, True), load_shares(number_of, rows * top, reach, lean, False)
    places = jnp.arange(number_of)

    def named(sizes, turn):
        used = int((sizes > 0).sum())
        fixed = max(1, used // 4)
        shifted = fixed + (places - fixed + turn * (used - fixed)) % max(1, number_of - fixed)
        return jnp.zeros((number_of,), jnp.int32).at[sequence[jnp.where(places < fixed, places, shifted)]].set(jnp.asarray(sizes, jnp.int32))

    sizes = jnp.where(number % 4 == 0, named(heavy_load, number // 4), named(common, number - number // 4 - 1))
    mixed = jax.random.permutation(jax.random.fold_in(own, 3), number_of)
    source_of, taker = mixed[0:number_of // 2 * 2:2], mixed[1:number_of // 2 * 2:2]
    slack = jnp.minimum(sizes[source_of] - 1, reach - sizes[taker]) // 2
    slack = jnp.where((source_of == sequence[0]) | (taker == sequence[0]) | (sizes[taker] == 0), 0, jnp.maximum(slack, 0))
    shifted = jax.random.randint(jax.random.fold_in(own, 4), (number_of // 2,), 0, 1 << 20) % (slack + 1)
    sizes = sizes.at[source_of].add(-shifted).at[taker].add(shifted)
    items = jnp.searchsorted(jnp.cumsum(sizes), jnp.arange(rows * top), side="right").astype(jnp.int32)
    listing = items.reshape(top, rows).T
    listing = listing[jax.random.permutation(jax.random.fold_in(own, 1), rows)]
    turn = jax.random.randint(jax.random.fold_in(own, 2), (rows, 1), 0, top)
    return jnp.take_along_axis(listing, (jnp.arange(top)[None, :] + turn) % top, axis=1)


def load_shares(amount, total, limit, lean, full):
    loads = [(1 << 20) // math.isqrt(standing ** lean) + 1 for standing in range(1, amount + 1)]
    largest = limit if full else min(limit, max(-(-total // amount), total * loads[0] // sum(loads)))
    least = 1 if total - largest >= amount - 1 else 0
    given, spare = [largest] + [least] * (amount - 1), total - largest - least * (amount - 1)
    while spare > 0:
        candidates = [i for i in range(1, amount) if given[i] < largest] or [i for i in range(1, amount) if given[i] < limit]
        whole, remaining = sum([loads[i] for i in candidates]), spare
        for i in candidates:
            extra = min(limit - given[i], max(1, remaining * loads[i] // whole), spare)
            given[i] = given[i] + extra
            spare = spare - extra
    return np.array(given)


def bell_draw(stream_key, shape, scale, bound, split=(), dtype=jnp.bfloat16):
    array = jax.random.normal(stream_key, shape, jnp.float32) * scale
    if len(split) > 0:
        array = block_scale(stream_key, shape, split, -0.22, 0.18) * array
    return jnp.clip(array, min=-bound, max=bound).astype(dtype)


def setup_inputs(seed: int = 0) -> dict:
    key_list = jax.random.split(jax.random.key(seed), 10)
    forward_input = bell_draw(key_list[0], (SECTIONS, TOKENS, D), 1.0, 6.0, ((0, 16), (1, 32)))
    backward_input = bell_draw(key_list[1], (SECTIONS, TOKENS, D), 1.0, 6.0, ((0, 16), (1, 32)))
    backward_grad = bell_draw(key_list[2], (SECTIONS, TOKENS, D), 1.0, 6.0, ((0, 16), (1, 32)))
    gate_up_weight = bell_draw(key_list[3], (SECTIONS, D, 2 * EXPERTS * HID), D ** -0.5, 0.09375, ((0, 16), (2, 32)))
    down_weight = bell_draw(key_list[4], (SECTIONS, EXPERTS * HID, D), HID ** -0.5, 0.1875, ((0, 16), (1, 32)))
    forward_routes_keys = jax.random.split(jax.random.fold_in(key_list[5], 1), SECTIONS * TOKENS // TOK_DEV)
    forward_routes_turns = jax.random.permutation(jax.random.fold_in(key_list[5], 3), SECTIONS * TOKENS // TOK_DEV)
    forward_routes = jax.vmap(lambda own, number: deal_out(jax.random.fold_in(key_list[5], 2), own, number, TOK_DEV, EXPERTS, TOPK, CAP, 2))(forward_routes_keys, forward_routes_turns).reshape((SECTIONS, TOKENS, TOPK))
    backward_routes_keys = jax.random.split(jax.random.fold_in(key_list[6], 1), SECTIONS * TOKENS // TOK_DEV)
    backward_routes_turns = jax.random.permutation(jax.random.fold_in(key_list[6], 3), SECTIONS * TOKENS // TOK_DEV)
    backward_routes = jax.vmap(lambda own, number: deal_out(jax.random.fold_in(key_list[6], 2), own, number, TOK_DEV, EXPERTS, TOPK, CAP, 2))(backward_routes_keys, backward_routes_turns).reshape((SECTIONS, TOKENS, TOPK))
    forward_gates = jnp.clip(jnp.exp(math.log(1.0) - 2.3025851 * jax.random.uniform(key_list[7], (SECTIONS, TOKENS, TOPK), jnp.float32) ** block_scale(key_list[7], (SECTIONS, TOKENS, TOPK), ((0, 16), (1, 32)), -0.2, 0.2)), 0.1, 1.0)
    backward_gates = jnp.clip(jnp.exp(math.log(1.0) - 2.3025851 * jax.random.uniform(key_list[8], (SECTIONS, TOKENS, TOPK), jnp.float32) ** block_scale(key_list[8], (SECTIONS, TOKENS, TOPK), ((0, 16), (1, 32)), -0.2, 0.2)), 0.1, 1.0)
    return dict(forward_input=forward_input, backward_input=backward_input, backward_grad=backward_grad, gate_up_weight=gate_up_weight, down_weight=down_weight, forward_routes=forward_routes, backward_routes=backward_routes, forward_gates=forward_gates, backward_gates=backward_gates)


def settle(values):
    return lax.optimization_barrier(values.astype(jnp.bfloat16)).astype(jnp.float32)


def expert_weight(routes, gate_share, expert_id):
    return jnp.sum(jnp.where(routes == expert_id, gate_share, 0.0), axis=1)


def section_forward(operands):
    tokens, gate_up, down, routes, gate_share = operands
    slices = N_EXPERT // EXPERTS
    part_width = HID // slices
    tables = gate_up.reshape(D, EXPERTS, slices, 2, part_width)
    down_tables = down.reshape(EXPERTS, slices, part_width, D)
    running = tokens.astype(jnp.float32)
    for expert_id in range(EXPERTS):
        gate_mat = tables[:, expert_id, :, 0, :].reshape(D, HID)
        up_mat = tables[:, expert_id, :, 1, :].reshape(D, HID)
        gate_val = jnp.dot(tokens, gate_mat, preferred_element_type=jnp.float32)
        up_val = jnp.dot(tokens, up_mat, preferred_element_type=jnp.float32)
        hidden = (jax.nn.silu(gate_val) * up_val).astype(jnp.bfloat16).reshape(-1, slices, part_width)
        pieces = jnp.einsum("tsh,shd->tsd", hidden.astype(jnp.float32), down_tables[expert_id].astype(jnp.float32), precision=lax.Precision.HIGHEST)
        pieces = settle(pieces)
        running = running + expert_weight(routes, gate_share, expert_id)[:, None] * jnp.sum(pieces, axis=1)
    return running.astype(jnp.bfloat16)


def section_backward(operands):
    tokens, upstream, gate_up, down, routes, gate_share = operands
    slices = N_EXPERT // EXPERTS
    part_width = HID // slices
    tables = gate_up.reshape(D, EXPERTS, slices, 2, part_width)
    down_tables = down.reshape(EXPERTS, slices, part_width, D)
    running = upstream.astype(jnp.float32)
    for expert_id in range(EXPERTS):
        gate_tab = tables[:, expert_id, :, 0, :]
        up_tab = tables[:, expert_id, :, 1, :]
        gate_val = jnp.dot(tokens, gate_tab.reshape(D, HID), preferred_element_type=jnp.float32).reshape(-1, slices, part_width)
        up_val = jnp.dot(tokens, up_tab.reshape(D, HID), preferred_element_type=jnp.float32).reshape(-1, slices, part_width)
        hidden_grad = jnp.einsum("td,shd->tsh", upstream.astype(jnp.float32), down_tables[expert_id].astype(jnp.float32), precision=lax.Precision.HIGHEST)
        sigmoid_val = jax.nn.sigmoid(gate_val)
        gate_grad = (hidden_grad * up_val * sigmoid_val * (1.0 + gate_val * (1.0 - sigmoid_val))).astype(jnp.bfloat16)
        up_grad = (hidden_grad * gate_val * sigmoid_val).astype(jnp.bfloat16)
        pieces = jnp.einsum("tsh,dsh->tsd", gate_grad.astype(jnp.float32), gate_tab.astype(jnp.float32), precision=lax.Precision.HIGHEST)
        pieces = pieces + jnp.einsum("tsh,dsh->tsd", up_grad.astype(jnp.float32), up_tab.astype(jnp.float32), precision=lax.Precision.HIGHEST)
        pieces = settle(pieces)
        running = running + expert_weight(routes, gate_share, expert_id)[:, None] * jnp.sum(pieces, axis=1)
    return running.astype(jnp.bfloat16)


def reference(forward_input, backward_input, backward_grad, gate_up_weight, down_weight, forward_routes, backward_routes, forward_gates, backward_gates):
    forward_out = lax.map(section_forward, (forward_input, gate_up_weight, down_weight, forward_routes, forward_gates))
    backward_out = lax.map(section_backward, (backward_input, backward_grad, gate_up_weight, down_weight, backward_routes, backward_gates))
    zero_block = jnp.zeros_like(forward_out[:1])
    forward_next = jnp.concatenate([zero_block, forward_out[:-1]], axis=0)
    backward_next = jnp.concatenate([backward_out[1:], zero_block], axis=0)
    return forward_next, backward_next
```

```python
import jax
import jax.numpy as jnp
from jax import lax
from jax.sharding import PartitionSpec as P

EXPERTS = 4
Z = 4
CORES = 2
LANES = 128


def expert_index(x, z, core):
    return (x * Z + z) * CORES + core


def expert_route(move):
    return [
        (expert_index(x, z, c), expert_index(*move(x, z, c)))
        for x in range(EXPERTS)
        for z in range(Z)
        for c in range(CORES)
    ]


def along_x(block, distance):
    route = expert_route(lambda x, z, c: ((x + distance) % EXPERTS, z, c))
    return lax.ppermute(block, "expert", route)


def along_z(block, distance):
    route = expert_route(lambda x, z, c: (x, (z + distance) % Z, c))
    return lax.ppermute(block, "expert", route)


def other_core(block):
    return lax.ppermute(block, "expert", expert_route(lambda x, z, c: (x, z, 1 - c)))


def to_section(block, step, distance):
    sections = lax.axis_size("pipe")
    width = EXPERTS * Z * CORES
    route = [
        (p * width + source, (p + step) * width + target)
        for p in range(sections)
        if 0 <= p + step < sections
        for source, target in expert_route(lambda x, z, c: (x, (z + distance) % Z, c))
    ]
    return lax.ppermute(block, ("pipe", "expert"), route)


def expert_shares(routes, gates):
    hot = routes[:, :, None] == jnp.arange(EXPERTS, dtype=jnp.int32)
    return jnp.sum(jnp.where(hot, gates[:, :, None], 0.0), axis=1)


def share_columns(shares):
    first = lax.reduce_precision(shares, 8, 7)
    second = lax.reduce_precision(shares - first, 8, 7)
    third = shares - first - second
    parts = jnp.concatenate([first, second, third], axis=1)
    parts = jnp.pad(parts, ((0, 0), (0, LANES - parts.shape[1])))
    return parts.astype(jnp.bfloat16)


def shares_of(columns, width):
    parts = columns.astype(jnp.float32)
    return parts[:, :width] + parts[:, width : 2 * width] + parts[:, 2 * width : 3 * width]


def dot(a, b):
    return jnp.dot(a, b, preferred_element_type=jnp.float32)


def dot_t(a, b):
    return lax.dot_general(a, b, (((1,), (1,)), ((), ())), preferred_element_type=jnp.float32)


def forward_rows(rows, gate_ups, down):
    hidden = []
    for gate_up in gate_ups:
        both = dot(rows, gate_up)
        gate_val, up_val = jnp.split(both, 2, axis=1)
        hidden.append((jax.nn.silu(gate_val) * up_val).astype(jnp.bfloat16))
    return dot(jnp.concatenate(hidden, axis=1), down).astype(jnp.bfloat16)


def backward_rows(rows, grads, gate_ups, down):
    hidden_grads = jnp.split(dot_t(grads, down), len(gate_ups), axis=1)
    total = None
    for gate_up, hidden_grad in zip(gate_ups, hidden_grads):
        both = dot(rows, gate_up)
        gate_val, up_val = jnp.split(both, 2, axis=1)
        sig = jax.nn.sigmoid(gate_val)
        gate_grad = hidden_grad * up_val * sig * (1.0 + gate_val * (1.0 - sig))
        up_grad = hidden_grad * gate_val * sig
        grad = jnp.concatenate([gate_grad, up_grad], axis=1).astype(jnp.bfloat16)
        term = dot_t(grad, gate_up)
        total = term if total is None else total + term
    return total.astype(jnp.bfloat16)


def gated_sum(parts, shares):
    me = lax.axis_index("expert") // (Z * CORES)
    total = 0.0
    for d, part in enumerate(parts):
        hot = jnp.arange(EXPERTS, dtype=jnp.int32) == lax.rem(me + d, EXPERTS)
        share = jnp.sum(jnp.where(hot[None, :], shares, 0.0), axis=1, keepdims=True)
        total = total + share * part.astype(jnp.float32)
    return total


def send_home(mixture, residual, step):
    rows = residual.shape[0]
    total = 0.0
    for k in range(Z):
        term = mixture[k * rows : (k + 1) * rows]
        if k == 0:
            term = term + residual.astype(jnp.float32)
        total = total + to_section(term.astype(jnp.bfloat16), step, -k).astype(jnp.float32)
    return total.astype(jnp.bfloat16)


def on_device(
    forward_input,
    backward_input,
    backward_grad,
    gate_up_weight,
    down_weight,
    forward_routes,
    backward_routes,
    forward_gates,
    backward_gates,
):
    tokens, saved, upstream = forward_input[0], backward_input[0], backward_grad[0]
    rows, model = tokens.shape
    shares = jnp.concatenate(
        [
            expert_shares(forward_routes[0], forward_gates[0]),
            expert_shares(backward_routes[0], backward_gates[0]),
        ],
        axis=1,
    )
    with jax.named_scope("gather_z"):
        first = jnp.concatenate([tokens, share_columns(shares)], axis=1)
        first = [first] + [along_z(first, d) for d in range(1, Z)]
        second = jnp.concatenate([saved, upstream], axis=0)
        second = [second] + [along_z(second, d) for d in range(1, Z)]
    with jax.named_scope("swap_weights"):
        gate_up, down = gate_up_weight[0], down_weight[0]
        gate_ups = [gate_up, other_core(gate_up)]
        down = jnp.concatenate([down, other_core(down)], axis=0)
    with jax.named_scope("gather_x"):
        forward_block = jnp.concatenate([part[:, :model] for part in first], axis=0)
        all_shares = jnp.concatenate([part[:, model:] for part in first], axis=0)
        all_shares = shares_of(all_shares, 2 * EXPERTS)
        forward_parts = [forward_block] + [along_x(forward_block, d) for d in range(1, EXPERTS)]
        backward_block = jnp.concatenate(
            [part[:rows] for part in second] + [part[rows:] for part in second], axis=0
        )
        backward_parts = [backward_block] + [along_x(backward_block, d) for d in range(1, EXPERTS)]
    half = Z * rows
    with jax.named_scope("forward_experts"):
        outs = [forward_rows(part, gate_ups, down) for part in forward_parts]
        outs = [outs[0]] + [along_x(outs[d], -d) for d in range(1, EXPERTS)]
        mixture = gated_sum(outs, all_shares[:, :EXPERTS])
        forward_next = send_home(mixture, tokens, 1)
    with jax.named_scope("backward_experts"):
        outs = [backward_rows(part[:half], part[half:], gate_ups, down) for part in backward_parts]
        outs = [outs[0]] + [along_x(outs[d], -d) for d in range(1, EXPERTS)]
        mixture = gated_sum(outs, all_shares[:, EXPERTS:])
        backward_next = send_home(mixture, upstream, -1)
    return (forward_next[None], backward_next[None])


def solution(mesh):
    by_token = P("pipe", "expert", None)
    return jax.shard_map(
        on_device,
        mesh=mesh,
        in_specs=(by_token,) * 3 + (P("pipe", None, "expert"),) + (by_token,) * 5,
        out_specs=(by_token, by_token),
        check_vma=False,
    )
```

```python
import jax
import jax.numpy as jnp
from jax import lax
from jax.sharding import PartitionSpec as P

EXPERTS = 4
Z = 4
CORES = 2
LANES = 128
CAP = 12


def expert_index(x, z, core):
    return (x * Z + z) * CORES + core


def expert_route(move):
    return [
        (expert_index(x, z, c), expert_index(*move(x, z, c)))
        for x in range(EXPERTS)
        for z in range(Z)
        for c in range(CORES)
    ]


def across_x(blocks):
    groups = [
        [expert_index(x, z, c) for x in range(EXPERTS)] for z in range(Z) for c in range(CORES)
    ]
    return lax.all_to_all(blocks, "expert", 0, 0, axis_index_groups=groups, tiled=True)


def along_z(block, distance):
    route = expert_route(lambda x, z, c: (x, (z + distance) % Z, c))
    return lax.ppermute(block, "expert", route)


def other_core(block):
    return lax.ppermute(block, "expert", expert_route(lambda x, z, c: (x, z, 1 - c)))


def to_section(block, step, distance):
    sections = lax.axis_size("pipe")
    width = EXPERTS * Z * CORES
    route = [
        (p * width + source, (p + step) * width + target)
        for p in range(sections)
        if 0 <= p + step < sections
        for source, target in expert_route(lambda x, z, c: (x, (z + distance) % Z, c))
    ]
    return lax.ppermute(block, ("pipe", "expert"), route)


def after(values, *others):
    return lax.optimization_barrier((values, others))[0]


def expert_hot(routes):
    return routes[:, :, None] == jnp.arange(EXPERTS, dtype=jnp.int32)


def expert_shares(hot, gates):
    return jnp.sum(jnp.where(hot, gates[:, :, None], 0.0), axis=1)


def expert_slots(hot):
    named = jnp.any(hot, axis=1)
    count = named.astype(jnp.int32)
    earlier = jnp.cumsum(count, axis=0) - count
    return jnp.where(named, earlier, -1).astype(jnp.float32)


def three_parts(values):
    first = lax.reduce_precision(values, 8, 7)
    second = lax.reduce_precision(values - first, 8, 7)
    return [part.astype(jnp.bfloat16) for part in (first, second, values - first - second)]


def side_columns(shares, slots):
    parts = jnp.concatenate(three_parts(shares) + [slots.astype(jnp.bfloat16)], axis=1)
    return jnp.pad(parts, ((0, 0), (0, LANES - parts.shape[1])))


def side_values(columns):
    width = 2 * EXPERTS
    parts = columns[:, : 4 * width].astype(jnp.float32)
    first, second, third, slots = jnp.split(parts, 4, axis=1)
    return first + second + third, slots


def placement(slots, rows):
    place = jnp.arange(EXPERTS * Z * CAP, dtype=jnp.int32)
    block = jnp.arange(slots.shape[0], dtype=jnp.int32) // rows
    expert, source, slot = place // (Z * CAP), place // CAP % Z, place % CAP
    wanted = jnp.repeat(slots, Z * CAP, axis=1)
    return (block[:, None] == source[None, :]) & (wanted == slot.astype(jnp.float32)[None, :])


def dot(a, b):
    return jnp.dot(a, b, preferred_element_type=jnp.float32)


def dot_t(a, b):
    return lax.dot_general(a, b, (((1,), (1,)), ((), ())), preferred_element_type=jnp.float32)


def pack(places, block):
    packed = lax.dot_general(
        places.astype(jnp.bfloat16),
        block,
        (((0,), (0,)), ((), ())),
        preferred_element_type=jnp.float32,
    )
    return packed.astype(jnp.bfloat16)


def forward_rows(rows, gate_ups, down):
    hidden = []
    for gate_up in gate_ups:
        both = dot(rows, gate_up)
        gate_val, up_val = jnp.split(both, 2, axis=1)
        hidden.append((jax.nn.silu(gate_val) * up_val).astype(jnp.bfloat16))
    return dot(jnp.concatenate(hidden, axis=1), down).astype(jnp.bfloat16)


def backward_rows(rows, grads, gate_ups, down):
    hidden_grads = jnp.split(dot_t(grads, down), len(gate_ups), axis=1)
    total = None
    for gate_up, hidden_grad in zip(gate_ups, hidden_grads):
        both = dot(rows, gate_up)
        gate_val, up_val = jnp.split(both, 2, axis=1)
        sig = jax.nn.sigmoid(gate_val)
        gate_grad = hidden_grad * up_val * sig * (1.0 + gate_val * (1.0 - sig))
        up_grad = hidden_grad * gate_val * sig
        grad = jnp.concatenate([gate_grad, up_grad], axis=1).astype(jnp.bfloat16)
        term = dot_t(grad, gate_up)
        total = term if total is None else total + term
    return total.astype(jnp.bfloat16)


def gated_sum(parts, places, shares):
    weights = jnp.where(places, jnp.repeat(shares, Z * CAP, axis=1), 0.0)
    return sum(dot(weight, parts) for weight in three_parts(weights))


def send_home(mixture, residual, step):
    rows = residual.shape[0]
    own = mixture[:rows] + residual.astype(jnp.float32)
    parts = [
        to_section(mixture[k * rows : (k + 1) * rows].astype(jnp.bfloat16), step, -k)
        for k in range(1, Z)
    ]
    total = to_section(own, step, 0)
    for part in parts:
        total = total + part.astype(jnp.float32)
    return total.astype(jnp.bfloat16)


def on_device(
    forward_input,
    backward_input,
    backward_grad,
    gate_up_weight,
    down_weight,
    forward_routes,
    backward_routes,
    forward_gates,
    backward_gates,
):
    tokens, saved, upstream = forward_input[0], backward_input[0], backward_grad[0]
    rows, model = tokens.shape
    with jax.named_scope("gather_z"):
        hots = [expert_hot(forward_routes[0]), expert_hot(backward_routes[0])]
        shares = [
            expert_shares(hots[0], forward_gates[0]),
            expert_shares(hots[1], backward_gates[0]),
        ]
        slots = [expert_slots(hot) for hot in hots]
        side = side_columns(jnp.concatenate(shares, axis=1), jnp.concatenate(slots, axis=1))
        mine = jnp.concatenate([tokens, saved, upstream, side], axis=1)
        parts = [mine] + [along_z(mine, d) for d in range(1, Z)]
    with jax.named_scope("swap_weights"):
        gate_up, down = gate_up_weight[0], down_weight[0]
        gate_ups = [gate_up, other_core(gate_up)]
        down_other = other_core(down)
        down = jnp.concatenate([down, down_other], axis=0)
    with jax.named_scope("gather_x"):
        block = jnp.concatenate([part[:, : 3 * model] for part in parts], axis=0)
        side = jnp.concatenate([part[:, 3 * model :] for part in parts], axis=0)
        shares, slots = side_values(side)
        places = placement(slots[:, :EXPERTS], rows)
        back_places = placement(slots[:, EXPERTS:], rows)
        packed = [pack(places, block[:, :model]), pack(back_places, block[:, model:])]
        inbound = across_x(jnp.concatenate(packed, axis=1))
    with jax.named_scope("experts"):
        outs = forward_rows(inbound[:, :model], gate_ups, down)
        back = backward_rows(
            inbound[:, model : 2 * model], inbound[:, 2 * model :], gate_ups, down
        )
        outs = across_x(jnp.concatenate([outs, back], axis=1))
    with jax.named_scope("home"):
        mixture = gated_sum(outs[:, :model], places, shares[:, :EXPERTS])
        forward_next = send_home(mixture, tokens, 1)
        mixture = gated_sum(outs[:, model:], back_places, shares[:, EXPERTS:])
        backward_next = send_home(mixture, upstream, -1)
    return (forward_next[None], backward_next[None])


def solution(mesh):
    by_token = P("pipe", "expert", None)
    return jax.shard_map(
        on_device,
        mesh=mesh,
        in_specs=(by_token,) * 3 + (P("pipe", None, "expert"),) + (by_token,) * 5,
        out_specs=(by_token, by_token),
        check_vma=False,
    )
```

```python
import jax
import jax.numpy as jnp
from jax import lax
from jax.sharding import PartitionSpec as P

EXPERTS = 4
Z = 4
CORES = 2
LANES = 128
CAP = 12
OWNERS = (0, -1, 1, -2)


def expert_index(x, z, core):
    return (x * Z + z) * CORES + core


def expert_route(move):
    return [
        (expert_index(x, z, c), expert_index(*move(x, z, c)))
        for x in range(EXPERTS)
        for z in range(Z)
        for c in range(CORES)
    ]


def across_x(blocks):
    groups = [
        [expert_index(x, z, c) for x in range(EXPERTS)] for z in range(Z) for c in range(CORES)
    ]
    return lax.all_to_all(blocks, "expert", 0, 0, axis_index_groups=groups, tiled=True)


def turn(core):
    return 1 - 2 * core


def along_z(block, distance):
    route = expert_route(lambda x, z, c: (x, (z + distance * turn(c)) % Z, c))
    return lax.ppermute(block, "expert", route)


def other_core(block):
    return lax.ppermute(block, "expert", expert_route(lambda x, z, c: (x, z, 1 - c)))


def to_section(block, step, distance):
    sections = lax.axis_size("pipe")
    width = EXPERTS * Z * CORES
    route = [
        (p * width + source, (p + step) * width + target)
        for p in range(sections)
        if 0 <= p + step < sections
        for source, target in expert_route(lambda x, z, c: (x, (z + distance * turn(c)) % Z, c))
    ]
    return lax.ppermute(block, ("pipe", "expert"), route)


def together(*values):
    return lax.optimization_barrier(values)


def expert_hot(routes):
    return routes[:, :, None] == jnp.arange(EXPERTS, dtype=jnp.int32)


def expert_shares(hot, gates):
    return jnp.sum(jnp.where(hot, gates[:, :, None], 0.0), axis=1)


def expert_slots(hot):
    named = jnp.any(hot, axis=1)
    count = named.astype(jnp.int32)
    earlier = jnp.cumsum(count, axis=0) - count
    return jnp.where(named, earlier, -1).astype(jnp.float32)


def three_parts(values):
    first = lax.reduce_precision(values, 8, 7)
    second = lax.reduce_precision(values - first, 8, 7)
    return [part.astype(jnp.bfloat16) for part in (first, second, values - first - second)]


def side_columns(shares, slots):
    parts = jnp.concatenate(three_parts(shares) + [slots.astype(jnp.bfloat16)], axis=1)
    return jnp.pad(parts, ((0, 0), (0, LANES - parts.shape[1])))


def side_values(columns):
    width = 2 * EXPERTS
    parts = columns[:, : 4 * width].astype(jnp.float32)
    first, second, third, slots = jnp.split(parts, 4, axis=1)
    return first + second + third, slots


def placement(slots, rows):
    place = jnp.arange(EXPERTS * Z * CAP, dtype=jnp.int32)
    block = jnp.arange(slots.shape[0], dtype=jnp.int32) // rows
    expert, source, slot = place // (Z * CAP), place // CAP % Z, place % CAP
    wanted = jnp.repeat(slots, Z * CAP, axis=1)
    return (block[:, None] == source[None, :]) & (wanted == slot.astype(jnp.float32)[None, :])


def dot(a, b):
    return jnp.dot(a, b, preferred_element_type=jnp.float32)


def dot_t(a, b):
    return lax.dot_general(a, b, (((1,), (1,)), ((), ())), preferred_element_type=jnp.float32)


def pack(places, block):
    packed = lax.dot_general(
        places.astype(jnp.bfloat16),
        block,
        (((0,), (0,)), ((), ())),
        preferred_element_type=jnp.float32,
    )
    return packed.astype(jnp.bfloat16)


def forward_rows(rows, gate_ups, down):
    hidden = []
    for gate_up in gate_ups:
        both = dot(rows, gate_up)
        gate_val, up_val = jnp.split(both, 2, axis=1)
        hidden.append((jax.nn.silu(gate_val) * up_val).astype(jnp.bfloat16))
    return dot(jnp.concatenate(hidden, axis=1), down).astype(jnp.bfloat16)


def backward_rows(rows, grads, gate_ups, down):
    hidden_grads = jnp.split(dot_t(grads, down), len(gate_ups), axis=1)
    total = None
    for gate_up, hidden_grad in zip(gate_ups, hidden_grads):
        both = dot(rows, gate_up)
        gate_val, up_val = jnp.split(both, 2, axis=1)
        sig = jax.nn.sigmoid(gate_val)
        gate_grad = hidden_grad * up_val * sig * (1.0 + gate_val * (1.0 - sig))
        up_grad = hidden_grad * gate_val * sig
        grad = jnp.concatenate([gate_grad, up_grad], axis=1).astype(jnp.bfloat16)
        term = dot_t(grad, gate_up)
        total = term if total is None else total + term
    return total.astype(jnp.bfloat16)


def gated_sum(parts, places, shares):
    weights = jnp.where(places, jnp.repeat(shares, Z * CAP, axis=1), 0.0)
    return sum(dot(weight, parts) for weight in three_parts(weights))


def send_home(mixture, residual, step):
    rows = residual.shape[0]
    own = mixture[:rows] + residual.astype(jnp.float32)
    parts = [
        to_section(mixture[k * rows : (k + 1) * rows].astype(jnp.bfloat16), step, distance)
        for k, distance in enumerate(OWNERS) if k > 0
    ]
    total = to_section(own, step, 0)
    for part in parts:
        total = total + part.astype(jnp.float32)
    return total.astype(jnp.bfloat16)


def on_device(
    forward_input,
    backward_input,
    backward_grad,
    gate_up_weight,
    down_weight,
    forward_routes,
    backward_routes,
    forward_gates,
    backward_gates,
):
    tokens, saved, upstream = forward_input[0], backward_input[0], backward_grad[0]
    rows, model = tokens.shape
    with jax.named_scope("gather_z"):
        hots = [expert_hot(forward_routes[0]), expert_hot(backward_routes[0])]
        shares = [
            expert_shares(hots[0], forward_gates[0]),
            expert_shares(hots[1], backward_gates[0]),
        ]
        slots = [expert_slots(hot) for hot in hots]
        side = side_columns(jnp.concatenate(shares, axis=1), jnp.concatenate(slots, axis=1))
        mine = jnp.concatenate([tokens, side], axis=1)
        near, far = along_z(mine, 1), along_z(mine, -1)
        gate_up, down = gate_up_weight[0], down_weight[0]
        gate_up_2, down_2 = other_core(gate_up), other_core(down)
        near, far, gate_up_2, down_2 = together(near, far, gate_up_2, down_2)
        back_mine = jnp.concatenate([saved, upstream], axis=1)
        both = along_z(jnp.concatenate([near, back_mine], axis=1), 1)
        both, back_far = together(both, along_z(back_mine, -1))
        opposite, back_near = both[:, : mine.shape[1]], both[:, mine.shape[1] :]
        parts = [mine, near, far, opposite]
        gate_ups, down = [gate_up, gate_up_2], jnp.concatenate([down, down_2], axis=0)
    with jax.named_scope("gather_x"):
        block = jnp.concatenate([part[:, :model] for part in parts], axis=0)
        shares, slots = side_values(jnp.concatenate([part[:, model:] for part in parts], axis=0))
        places = placement(slots[:, :EXPERTS], rows)
        back_places = placement(slots[:, EXPERTS:], rows)
        token_rows = across_x(pack(places, block))
        token_rows, back_opposite = together(token_rows, along_z(back_near, 1))
        back_block = jnp.concatenate([back_mine, back_near, back_far, back_opposite], axis=0)
        back_rows = across_x(pack(back_places, back_block))
    with jax.named_scope("forward_experts"):
        outs = forward_rows(token_rows, gate_ups, down)
        outs, back_rows = together(outs, back_rows)
        outs = across_x(outs)
    with jax.named_scope("backward_experts"):
        back_outs = backward_rows(back_rows[:, :model], back_rows[:, model:], gate_ups, down)
        back_outs = across_x(back_outs)
    with jax.named_scope("forward_home"):
        mixture = gated_sum(outs, places, shares[:, :EXPERTS])
        forward_next = send_home(mixture, tokens, 1)
    with jax.named_scope("backward_home"):
        mixture = gated_sum(back_outs, back_places, shares[:, EXPERTS:])
        backward_next = send_home(mixture, upstream, -1)
    return (forward_next[None], backward_next[None])


def solution(mesh):
    by_token = P("pipe", "expert", None)
    return jax.shard_map(
        on_device,
        mesh=mesh,
        in_specs=(by_token,) * 3 + (P("pipe", None, "expert"),) + (by_token,) * 5,
        out_specs=(by_token, by_token),
        check_vma=False,
    )
```

```python
import jax
import jax.numpy as jnp
from jax import lax
from jax.sharding import PartitionSpec as P

EXPERTS = 4
Z = 4
CORES = 2
LANES = 128
CAP = 12
OWNERS = (0, -1, 1, -2)
REACH = (1, -1, 2)


def expert_index(x, z, core):
    return (x * Z + z) * CORES + core


def expert_route(move):
    return [
        (expert_index(x, z, c), expert_index(*move(x, z, c)))
        for x in range(EXPERTS)
        for z in range(Z)
        for c in range(CORES)
    ]


def turn(core):
    return 1 - 2 * core


def along_z(block, distance):
    route = expert_route(lambda x, z, c: (x, (z + distance * turn(c)) % Z, c))
    return lax.ppermute(block, "expert", route)


def along_x(block, distance):
    route = expert_route(lambda x, z, c: ((x + distance * turn(c)) % EXPERTS, z, c))
    return lax.ppermute(block, "expert", route)


def other_core(block):
    return lax.ppermute(block, "expert", expert_route(lambda x, z, c: (x, z, 1 - c)))


def to_section(block, step, distance):
    sections = lax.axis_size("pipe")
    width = EXPERTS * Z * CORES
    route = [
        (p * width + source, (p + step) * width + target)
        for p in range(sections)
        if 0 <= p + step < sections
        for source, target in expert_route(lambda x, z, c: (x, (z + distance * turn(c)) % Z, c))
    ]
    return lax.ppermute(block, ("pipe", "expert"), route)


def together(*values):
    return lax.optimization_barrier(values)


def expert_hot(routes):
    return routes[:, :, None] == jnp.arange(EXPERTS, dtype=jnp.int32)


def expert_shares(hot, gates):
    return jnp.sum(jnp.where(hot, gates[:, :, None], 0.0), axis=1)


def expert_slots(hot):
    named = jnp.any(hot, axis=1)
    count = named.astype(jnp.int32)
    earlier = jnp.cumsum(count, axis=0) - count
    return jnp.where(named, earlier, -1).astype(jnp.float32)


def three_parts(values):
    first = lax.reduce_precision(values, 8, 7)
    second = lax.reduce_precision(values - first, 8, 7)
    return [part.astype(jnp.bfloat16) for part in (first, second, values - first - second)]


def side_columns(shares, slots):
    parts = jnp.concatenate(three_parts(shares) + [slots.astype(jnp.bfloat16)], axis=1)
    return jnp.pad(parts, ((0, 0), (0, LANES - parts.shape[1])))


def side_values(columns):
    width = 2 * EXPERTS
    parts = columns[:, : 4 * width].astype(jnp.float32)
    first, second, third, slots = jnp.split(parts, 4, axis=1)
    return first + second + third, slots


def column_of(table, index):
    hot = jnp.arange(table.shape[1], dtype=jnp.int32) == index
    return jnp.sum(jnp.where(hot[None, :], table, 0.0), axis=1, keepdims=True)


def placement(slots, expert, rows):
    slot = column_of(slots, expert)
    block = jnp.arange(slots.shape[0], dtype=jnp.int32) // rows
    place = jnp.arange(Z * CAP, dtype=jnp.int32)
    wanted = (place % CAP).astype(jnp.float32)
    found = (block[:, None] == place[None, :] // CAP) & (slot == wanted[None, :])
    return found.astype(jnp.bfloat16)


def dot(a, b):
    return jnp.dot(a, b, preferred_element_type=jnp.float32)


def dot_t(a, b):
    return lax.dot_general(a, b, (((1,), (1,)), ((), ())), preferred_element_type=jnp.float32)


def pack(places, block):
    packed = lax.dot_general(
        places,
        block,
        (((0,), (0,)), ((), ())),
        preferred_element_type=jnp.float32,
    )
    return packed.astype(jnp.bfloat16)


def forward_rows(rows, gate_ups, down):
    hidden = []
    for gate_up in gate_ups:
        both = dot(rows, gate_up)
        gate_val, up_val = jnp.split(both, 2, axis=1)
        hidden.append((jax.nn.silu(gate_val) * up_val).astype(jnp.bfloat16))
    return dot(jnp.concatenate(hidden, axis=1), down)


def backward_rows(rows, grads, gate_ups, down):
    hidden_grads = jnp.split(dot_t(grads, down), len(gate_ups), axis=1)
    total = None
    for gate_up, hidden_grad in zip(gate_ups, hidden_grads):
        both = dot(rows, gate_up)
        gate_val, up_val = jnp.split(both, 2, axis=1)
        sig = jax.nn.sigmoid(gate_val)
        gate_grad = hidden_grad * up_val * sig * (1.0 + gate_val * (1.0 - sig))
        up_grad = hidden_grad * gate_val * sig
        grad = jnp.concatenate([gate_grad, up_grad], axis=1).astype(jnp.bfloat16)
        term = dot_t(grad, gate_up)
        total = term if total is None else total + term
    return total


def gated_sum(own, parts, places, shares, experts):
    total = column_of(shares, experts[0]) * own
    for part, place, expert in zip(parts, places, experts[1:]):
        total = total + column_of(shares, expert) * dot(place, part)
    return total


def send_home(mixture, residual, step):
    rows = residual.shape[0]
    own = mixture[:rows] + residual.astype(jnp.float32)
    parts = [
        to_section(mixture[k * rows : (k + 1) * rows].astype(jnp.bfloat16), step, distance)
        for k, distance in enumerate(OWNERS) if k > 0
    ]
    total = to_section(own, step, 0)
    for part in parts:
        total = total + part.astype(jnp.float32)
    return total.astype(jnp.bfloat16)


def on_device(
    forward_input,
    backward_input,
    backward_grad,
    gate_up_weight,
    down_weight,
    forward_routes,
    backward_routes,
    forward_gates,
    backward_gates,
):
    tokens, saved, upstream = forward_input[0], backward_input[0], backward_grad[0]
    rows, model = tokens.shape
    core = lax.axis_index("expert") % CORES
    me = lax.axis_index("expert") // (Z * CORES)
    experts = [(me + EXPERTS + d * (1 - 2 * core)) % EXPERTS for d in (0,) + REACH]

    with jax.named_scope("gather_z"):
        near, far = along_z(tokens, 1), along_z(tokens, -1)
        hots = [expert_hot(forward_routes[0]), expert_hot(backward_routes[0])]
        shares = [
            expert_shares(hots[0], forward_gates[0]),
            expert_shares(hots[1], backward_gates[0]),
        ]
        slots = [expert_slots(hot) for hot in hots]
        side = side_columns(jnp.concatenate(shares, axis=1), jnp.concatenate(slots, axis=1))
        sides = [side] + [along_z(side, d) for d in (1, -1, 2)]
        near, far, *sides = together(near, far, *sides)
        shares, slots = side_values(jnp.concatenate(sides, axis=0))
        places = [placement(slots[:, :EXPERTS], e, rows) for e in experts[1:]]
        back_places = [placement(slots[:, EXPERTS:], e, rows) for e in experts[1:]]
        back_mine = jnp.concatenate([saved, upstream], axis=1)
        both = along_z(jnp.concatenate([near, back_mine], axis=1), 1)
        back_far = along_z(back_mine, -1)
    with jax.named_scope("swap_weights"):
        gate_up, down, near = together(gate_up_weight[0], down_weight[0], near)
        gate_up_2, down_2 = other_core(gate_up), other_core(down)
        both, back_far, gate_up_2, down_2 = together(both, back_far, gate_up_2, down_2)
        gate_ups, down = [gate_up, gate_up_2], jnp.concatenate([down, down_2], axis=0)
    with jax.named_scope("gather_x_forward"):
        opposite, back_near = both[:, :model], both[:, model:]
        block = jnp.concatenate([tokens, near, far, opposite], axis=0)
        parts = [along_x(pack(place, block), d) for place, d in zip(places, REACH)]
        *parts, back_opposite = together(*parts, along_z(back_near, 1))
    with jax.named_scope("gather_x_backward"):
        back_block = jnp.concatenate([back_mine, back_near, back_far, back_opposite], axis=0)
        back_parts = [pack(place, back_block) for place in back_places]
        *parts, back_1, back_2, back_3 = together(*parts, *back_parts)
        back_parts = [along_x(part, d) for part, d in zip((back_1, back_2, back_3), REACH)]
    with jax.named_scope("forward_experts"):
        own = forward_rows(block, gate_ups, down)
        outs = [forward_rows(part, gate_ups, down).astype(jnp.bfloat16) for part in parts]
        *outs, back_parts[0] = together(*outs, back_parts[0])
        outs = [along_x(out, -d) for out, d in zip(outs, REACH)]
    with jax.named_scope("backward_experts"):
        back_own = backward_rows(back_block[:, :model], back_block[:, model:], gate_ups, down)
        back_outs = [
            backward_rows(part[:, :model], part[:, model:], gate_ups, down).astype(jnp.bfloat16)
            for part in back_parts
        ]
        back_outs = [along_x(out, -d) for out, d in zip(back_outs, REACH)]
    with jax.named_scope("forward_home"):
        mixture = gated_sum(own, outs, places, shares[:, :EXPERTS], experts)
        forward_next = send_home(mixture, tokens, 1)
    with jax.named_scope("backward_home"):
        mixture = gated_sum(back_own, back_outs, back_places, shares[:, EXPERTS:], experts)
        backward_next = send_home(mixture, upstream, -1)
    return (forward_next[None], backward_next[None])


def solution(mesh):
    by_token = P("pipe", "expert", None)
    return jax.shard_map(
        on_device,
        mesh=mesh,
        in_specs=(by_token,) * 3 + (P("pipe", None, "expert"),) + (by_token,) * 5,
        out_specs=(by_token, by_token),
        check_vma=False,
    )
```

```python
import jax
import jax.numpy as jnp
from jax import lax
from jax.sharding import PartitionSpec as P

EXPERTS = 4
Z = 4
CORES = 2
LANES = 128


def expert_index(x, z, core):
    return (x * Z + z) * CORES + core


def expert_route(move):
    return [
        (expert_index(x, z, c), expert_index(*move(x, z, c)))
        for x in range(EXPERTS)
        for z in range(Z)
        for c in range(CORES)
    ]


def turn(core):
    return 1 - 2 * core


def gather_z(block):
    groups = [
        [expert_index(x, z, c) for z in range(Z)] for x in range(EXPERTS) for c in range(CORES)
    ]
    blocks = jnp.broadcast_to(block[None], (Z,) + block.shape)
    blocks = lax.all_to_all(blocks, "expert", 0, 0, axis_index_groups=groups, tiled=True)
    return blocks.reshape(Z * block.shape[0], block.shape[1])


def along_x(block, distance):
    route = expert_route(lambda x, z, c: ((x + distance * turn(c)) % EXPERTS, z, c))
    return lax.ppermute(block, "expert", route)


def other_core(block):
    return lax.ppermute(block, "expert", expert_route(lambda x, z, c: (x, z, 1 - c)))


def to_section(block, step, distance):
    sections = lax.axis_size("pipe")
    width = EXPERTS * Z * CORES
    route = [
        (p * width + source, (p + step) * width + target)
        for p in range(sections)
        if 0 <= p + step < sections
        for source, target in expert_route(lambda x, z, c: (x, (z + distance * turn(c)) % Z, c))
    ]
    return lax.ppermute(block, ("pipe", "expert"), route)


def together(*values):
    return lax.optimization_barrier(values)


def expert_hot(routes):
    return routes[:, :, None] == jnp.arange(EXPERTS, dtype=jnp.int32)


def expert_shares(hot, gates):
    return jnp.sum(jnp.where(hot, gates[:, :, None], 0.0), axis=1)


def three_parts(values):
    first = lax.reduce_precision(values, 8, 7)
    second = lax.reduce_precision(values - first, 8, 7)
    return [part.astype(jnp.bfloat16) for part in (first, second, values - first - second)]


def side_columns(shares):
    parts = jnp.concatenate(three_parts(shares), axis=1)
    return jnp.pad(parts, ((0, 0), (0, LANES - parts.shape[1])))


def side_values(columns):
    width = 2 * EXPERTS
    first, second, third = jnp.split(columns[:, : 3 * width].astype(jnp.float32), 3, axis=1)
    return first + second + third


def column_of(table, index):
    hot = jnp.arange(table.shape[1], dtype=jnp.int32) == index
    return jnp.sum(jnp.where(hot[None, :], table, 0.0), axis=1, keepdims=True)


def dot(a, b):
    return jnp.dot(a, b, preferred_element_type=jnp.float32)


def dot_t(a, b):
    return lax.dot_general(a, b, (((1,), (1,)), ((), ())), preferred_element_type=jnp.float32)


def forward_rows(rows, gate_up, down):
    gate_val, up_val = jnp.split(dot(rows, gate_up), 2, axis=1)
    hidden = (jax.nn.silu(gate_val) * up_val).astype(jnp.bfloat16)
    return dot(hidden, down)


def backward_rows(rows, grads, gate_up, down):
    hidden_grad = dot_t(grads, down)
    gate_val, up_val = jnp.split(dot(rows, gate_up), 2, axis=1)
    sig = jax.nn.sigmoid(gate_val)
    gate_grad = hidden_grad * up_val * sig * (1.0 + gate_val * (1.0 - sig))
    up_grad = hidden_grad * gate_val * sig
    grad = jnp.concatenate([gate_grad, up_grad], axis=1).astype(jnp.bfloat16)
    return dot_t(grad, gate_up)


def send_home(mixture, residual, step, place, turned):
    rows = residual.shape[0]
    total = 0.0
    for distance in (0, 1, -1, 2):
        owner = (place + Z + distance * turned) % Z
        block = lax.dynamic_slice_in_dim(mixture, owner * rows, rows, axis=0)
        if distance == 0:
            part = to_section(block + residual.astype(jnp.float32), step, 0)
        else:
            part = to_section(block.astype(jnp.bfloat16), step, distance)
        total = total + part.astype(jnp.float32)
    return total.astype(jnp.bfloat16)


def on_device(
    forward_input,
    backward_input,
    backward_grad,
    gate_up_weight,
    down_weight,
    forward_routes,
    backward_routes,
    forward_gates,
    backward_gates,
):
    tokens, saved, upstream = forward_input[0], backward_input[0], backward_grad[0]
    rows, model = tokens.shape
    index = lax.axis_index("expert")
    turned = 1 - 2 * (index % CORES)
    place = index // CORES % Z
    me = index // (Z * CORES)
    experts = [(me + EXPERTS + d * turned) % EXPERTS for d in (0, -1, 1, -2)]

    with jax.named_scope("gather_weights"):
        gate_up, down = gate_up_weight[0], down_weight[0]
        near = [along_x(gate_up, 1), along_x(gate_up, -1), along_x(down, 1), along_x(down, -1)]
    with jax.named_scope("gather_rows"):
        shares = [
            expert_shares(expert_hot(forward_routes[0]), forward_gates[0]),
            expert_shares(expert_hot(backward_routes[0]), backward_gates[0]),
        ]
        side = side_columns(jnp.concatenate(shares, axis=1))
        mine = gather_z(jnp.concatenate([tokens, saved, upstream, side], axis=1))
        mine, *near = together(mine, *near)
        gate_ups = [gate_up, near[0], near[1], along_x(near[0], 1)]
        downs = [down, near[2], near[3], along_x(near[2], 1)]
        both = [mine, other_core(mine)]
        cuts = (0, model, 2 * model, 3 * model, 3 * model + LANES)
        token_rows, saved_rows, upstream_rows, sides = [
            jnp.concatenate([part[:, low:high] for part in both], axis=0)
            for low, high in zip(cuts, cuts[1:])
        ]
        shares = side_values(sides)
    with jax.named_scope("experts"):
        forward_sum = backward_sum = 0.0
        for expert, gate_up, down in zip(experts, gate_ups, downs):
            out = forward_rows(token_rows, gate_up, down)
            forward_sum = forward_sum + column_of(shares[:, :EXPERTS], expert) * out
            out = backward_rows(saved_rows, upstream_rows, gate_up, down)
            backward_sum = backward_sum + column_of(shares[:, EXPERTS:], expert) * out
    half = Z * rows
    with jax.named_scope("forward_home"):
        other = other_core(forward_sum[half:].astype(jnp.bfloat16)).astype(jnp.float32)
        mixture = forward_sum[:half] + other
        forward_next = send_home(mixture, tokens, 1, place, turned)
    with jax.named_scope("backward_home"):
        other = other_core(backward_sum[half:].astype(jnp.bfloat16)).astype(jnp.float32)
        mixture = backward_sum[:half] + other
        backward_next = send_home(mixture, upstream, -1, place, turned)
    return (forward_next[None], backward_next[None])


def solution(mesh):
    by_token = P("pipe", "expert", None)
    return jax.shard_map(
        on_device,
        mesh=mesh,
        in_specs=(by_token,) * 3 + (P("pipe", None, "expert"),) + (by_token,) * 5,
        out_specs=(by_token, by_token),
        check_vma=False,
    )
```

```python
import jax
import jax.numpy as jnp
from jax import lax
from jax.sharding import PartitionSpec as P

EXPERTS = 4
Z = 4
CORES = 2
LANES = 128


def expert_index(x, z, core):
    return (x * Z + z) * CORES + core


def expert_route(move):
    return [
        (expert_index(x, z, c), expert_index(*move(x, z, c)))
        for x in range(EXPERTS)
        for z in range(Z)
        for c in range(CORES)
    ]


def turn(core):
    return 1 - 2 * core


def along_z(block, distance):
    route = expert_route(lambda x, z, c: (x, (z + distance * turn(c)) % Z, c))
    return lax.ppermute(block, "expert", route)


def along_x(block, distance):
    route = expert_route(lambda x, z, c: ((x + distance * turn(c)) % EXPERTS, z, c))
    return lax.ppermute(block, "expert", route)


def other_core(block):
    return lax.ppermute(block, "expert", expert_route(lambda x, z, c: (x, z, 1 - c)))


def to_section(block, step, distance):
    sections = lax.axis_size("pipe")
    width = EXPERTS * Z * CORES
    route = [
        (p * width + source, (p + step) * width + target)
        for p in range(sections)
        if 0 <= p + step < sections
        for source, target in expert_route(lambda x, z, c: (x, (z + distance * turn(c)) % Z, c))
    ]
    return lax.ppermute(block, ("pipe", "expert"), route)


def together(*values):
    return lax.optimization_barrier(values)


def expert_hot(routes):
    return routes[:, :, None] == jnp.arange(EXPERTS, dtype=jnp.int32)


def expert_shares(hot, gates):
    return jnp.sum(jnp.where(hot, gates[:, :, None], 0.0), axis=1)


def three_parts(values):
    first = lax.reduce_precision(values, 8, 7)
    second = lax.reduce_precision(values - first, 8, 7)
    return [part.astype(jnp.bfloat16) for part in (first, second, values - first - second)]


def side_columns(shares):
    parts = jnp.concatenate(three_parts(shares), axis=1)
    return jnp.pad(parts, ((0, 0), (0, LANES - parts.shape[1])))


def side_values(columns):
    width = 2 * EXPERTS
    first, second, third = jnp.split(columns[:, : 3 * width].astype(jnp.float32), 3, axis=1)
    return first + second + third


def column_of(table, index):
    hot = jnp.arange(table.shape[1], dtype=jnp.int32) == index
    return jnp.sum(jnp.where(hot[None, :], table, 0.0), axis=1, keepdims=True)


def dot(a, b):
    return jnp.dot(a, b, preferred_element_type=jnp.float32)


def dot_t(a, b):
    return lax.dot_general(a, b, (((1,), (1,)), ((), ())), preferred_element_type=jnp.float32)


def forward_rows(rows, gate_up, down):
    gate_val, up_val = jnp.split(dot(rows, gate_up), 2, axis=1)
    hidden = (jax.nn.silu(gate_val) * up_val).astype(jnp.bfloat16)
    return dot_t(hidden, down)


def backward_rows(rows, grads, gate_up, down):
    hidden_grad = dot(grads, down)
    gate_val, up_val = jnp.split(dot(rows, gate_up), 2, axis=1)
    sig = jax.nn.sigmoid(gate_val)
    gate_grad = hidden_grad * up_val * sig * (1.0 + gate_val * (1.0 - sig))
    up_grad = hidden_grad * gate_val * sig
    grad = jnp.concatenate([gate_grad, up_grad], axis=1).astype(jnp.bfloat16)
    return dot_t(grad, gate_up)


def send_home(mixture, residual, passed, step):
    own, near, far = jnp.split(mixture, Z, axis=0)[:3]
    near = near + passed.astype(jnp.float32)
    total = to_section(own + residual.astype(jnp.float32), step, 0)
    total = total + to_section(far.astype(jnp.bfloat16), step, 1).astype(jnp.float32)
    total = total + to_section(near.astype(jnp.bfloat16), step, -1).astype(jnp.float32)
    return total.astype(jnp.bfloat16)


def on_device(
    forward_input,
    backward_input,
    backward_grad,
    gate_up_weight,
    down_weight,
    forward_routes,
    backward_routes,
    forward_gates,
    backward_gates,
):
    tokens, saved, upstream = forward_input[0], backward_input[0], backward_grad[0]
    rows, model = tokens.shape
    index = lax.axis_index("expert")
    turned = 1 - 2 * (index % CORES)
    me = index // (Z * CORES)
    experts = [(me + EXPERTS + d * turned) % EXPERTS for d in (0, -1, 1, -2)]

    with jax.named_scope("gather_weights"):
        weights = jnp.concatenate([gate_up_weight[0], down_weight[0].T], axis=1)
        near, far = along_x(weights, 1), along_x(weights, -1)
    with jax.named_scope("gather_rows"):
        shares = [
            expert_shares(expert_hot(forward_routes[0]), forward_gates[0]),
            expert_shares(expert_hot(backward_routes[0]), backward_gates[0]),
        ]
        side = side_columns(jnp.concatenate(shares, axis=1))
        mine = jnp.concatenate([tokens, saved, upstream, side], axis=1)
        below, above = along_z(mine, 1), along_z(mine, -1)
        opposite = along_z(below, 1)
    with jax.named_scope("gather_opposite"):
        near, far, below, above, opposite = together(near, far, below, above, opposite)
        weights = [weights, near, far, along_x(near, 1)]
        mine = jnp.concatenate([mine, below, above, opposite], axis=0)
        both = [mine, other_core(mine)]
        cuts = (0, model, 2 * model, 3 * model, 3 * model + LANES)
        token_rows, saved_rows, upstream_rows, sides = [
            jnp.concatenate([part[:, low:high] for part in both], axis=0)
            for low, high in zip(cuts, cuts[1:])
        ]
        shares = side_values(sides)
    with jax.named_scope("experts"):
        forward_sum = backward_sum = 0.0
        width = gate_up_weight.shape[2]
        for expert, weight in zip(experts, weights):
            gate_up, down = weight[:, :width], weight[:, width:]
            out = forward_rows(token_rows, gate_up, down)
            forward_sum = forward_sum + column_of(shares[:, :EXPERTS], expert) * out
            out = backward_rows(saved_rows, upstream_rows, gate_up, down)
            backward_sum = backward_sum + column_of(shares[:, EXPERTS:], expert) * out
    half = Z * rows
    with jax.named_scope("cores"):
        others = [
            other_core(total[half:].astype(jnp.bfloat16)) for total in (forward_sum, backward_sum)
        ]
        mixture = forward_sum[:half] + others[0].astype(jnp.float32)
        back_mixture = backward_sum[:half] + others[1].astype(jnp.float32)
    with jax.named_scope("home"):
        passed = [total[half - rows :] for total in (mixture, back_mixture)]
        passed = along_z(jnp.concatenate(passed, axis=1).astype(jnp.bfloat16), -1)
        forward_next = send_home(mixture, tokens, passed[:, :model], 1)
        backward_next = send_home(back_mixture, upstream, passed[:, model:], -1)
    return (forward_next[None], backward_next[None])


def solution(mesh):
    by_token = P("pipe", "expert", None)
    return jax.shard_map(
        on_device,
        mesh=mesh,
        in_specs=(by_token,) * 3 + (P("pipe", None, "expert"),) + (by_token,) * 5,
        out_specs=(by_token, by_token),
        check_vma=False,
    )
```

```python
import jax
import jax.numpy as jnp
from jax import lax
from jax.sharding import PartitionSpec as P

EXPERTS = 4
Z = 4
CORES = 2
LANES = 128


def expert_index(x, z, core):
    return (x * Z + z) * CORES + core


def expert_route(move):
    return [
        (expert_index(x, z, c), expert_index(*move(x, z, c)))
        for x in range(EXPERTS)
        for z in range(Z)
        for c in range(CORES)
    ]


def turn(core):
    return 1 - 2 * core


def along_z(block, distance):
    route = expert_route(lambda x, z, c: (x, (z + distance * turn(c)) % Z, c))
    return lax.ppermute(block, "expert", route)


def along_x(block, distance):
    route = expert_route(lambda x, z, c: ((x + distance * turn(c)) % EXPERTS, z, c))
    return lax.ppermute(block, "expert", route)


def other_core(block):
    return lax.ppermute(block, "expert", expert_route(lambda x, z, c: (x, z, 1 - c)))


def to_section(block, step, distance):
    sections = lax.axis_size("pipe")
    width = EXPERTS * Z * CORES
    route = [
        (p * width + source, (p + step) * width + target)
        for p in range(sections)
        if 0 <= p + step < sections
        for source, target in expert_route(lambda x, z, c: (x, (z + distance * turn(c)) % Z, c))
    ]
    return lax.ppermute(block, ("pipe", "expert"), route)


def together(*values):
    return lax.optimization_barrier(values)


def expert_hot(routes):
    return routes[:, :, None] == jnp.arange(EXPERTS, dtype=jnp.int32)


def expert_shares(hot, gates):
    return jnp.sum(jnp.where(hot, gates[:, :, None], 0.0), axis=1)


def three_parts(values):
    first = lax.reduce_precision(values, 8, 7)
    second = lax.reduce_precision(values - first, 8, 7)
    return [part.astype(jnp.bfloat16) for part in (first, second, values - first - second)]


def side_columns(shares):
    parts = jnp.concatenate(three_parts(shares), axis=1)
    return jnp.pad(parts, ((0, 0), (0, LANES - parts.shape[1])))


def side_values(columns):
    width = 2 * EXPERTS
    first, second, third = jnp.split(columns[:, : 3 * width].astype(jnp.float32), 3, axis=1)
    return first + second + third


def column_of(table, index):
    hot = jnp.arange(table.shape[1], dtype=jnp.int32) == index
    return jnp.sum(jnp.where(hot[None, :], table, 0.0), axis=1, keepdims=True)


def dot(a, b):
    return jnp.dot(a, b, preferred_element_type=jnp.float32)


def dot_t(a, b):
    return lax.dot_general(a, b, (((1,), (1,)), ((), ())), preferred_element_type=jnp.float32)


def forward_rows(rows, gate_up, down):
    gate_val, up_val = jnp.split(dot(rows, gate_up), 2, axis=1)
    hidden = (jax.nn.silu(gate_val) * up_val).astype(jnp.bfloat16)
    return dot(hidden, down)


def backward_rows(rows, grads, gate_up, down):
    hidden_grad = dot_t(grads, down)
    gate_val, up_val = jnp.split(dot(rows, gate_up), 2, axis=1)
    sig = jax.nn.sigmoid(gate_val)
    gate_grad = hidden_grad * up_val * sig * (1.0 + gate_val * (1.0 - sig))
    up_grad = hidden_grad * gate_val * sig
    grad = jnp.concatenate([gate_grad, up_grad], axis=1).astype(jnp.bfloat16)
    return dot_t(grad, gate_up)


def send_home(mixture, residual, passed, step):
    own, near, far = jnp.split(mixture, Z, axis=0)[:3]
    near = near + passed.astype(jnp.float32)
    total = to_section(own + residual.astype(jnp.float32), step, 0)
    total = total + to_section(far.astype(jnp.bfloat16), step, 1).astype(jnp.float32)
    total = total + to_section(near.astype(jnp.bfloat16), step, -1).astype(jnp.float32)
    return total.astype(jnp.bfloat16)


def on_device(
    forward_input,
    backward_input,
    backward_grad,
    gate_up_weight,
    down_weight,
    forward_routes,
    backward_routes,
    forward_gates,
    backward_gates,
):
    tokens, saved, upstream = forward_input[0], backward_input[0], backward_grad[0]
    rows, model = tokens.shape
    index = lax.axis_index("expert")
    turned = 1 - 2 * (index % CORES)
    me = index // (Z * CORES)
    experts = [(me + EXPERTS + d * turned) % EXPERTS for d in (0, -1, 1, -2)]

    with jax.named_scope("gather_weights"):
        gate_up, down = gate_up_weight[0], down_weight[0]
        near = [along_x(gate_up, 1), along_x(gate_up, -1), along_x(down, 1), along_x(down, -1)]
    with jax.named_scope("gather_rows"):
        shares = [
            expert_shares(expert_hot(forward_routes[0]), forward_gates[0]),
            expert_shares(expert_hot(backward_routes[0]), backward_gates[0]),
        ]
        side = side_columns(jnp.concatenate(shares, axis=1))
        mine = jnp.concatenate([tokens, saved, upstream, side], axis=1)
        below, above = along_z(mine, 1), along_z(mine, -1)
        opposite = along_z(mine, 2)
    with jax.named_scope("gather_opposite"):
        mine = jnp.concatenate([mine, below, above, opposite], axis=0)
        mine, *near = together(mine, *near)
        gate_ups = [gate_up, near[0], near[1], along_x(near[0], 1)]
        downs = [down, near[2], near[3], along_x(near[2], 1)]
        both = [mine, other_core(mine)]
        cuts = (0, model, 2 * model, 3 * model, 3 * model + LANES)
        token_rows, saved_rows, upstream_rows, sides = [
            jnp.concatenate([part[:, low:high] for part in both], axis=0)
            for low, high in zip(cuts, cuts[1:])
        ]
        shares = side_values(sides)
    with jax.named_scope("experts"):
        forward_sum = backward_sum = 0.0
        for expert, gate_up, down in zip(experts, gate_ups, downs):
            out = forward_rows(token_rows, gate_up, down)
            forward_sum = forward_sum + column_of(shares[:, :EXPERTS], expert) * out
            out = backward_rows(saved_rows, upstream_rows, gate_up, down)
            backward_sum = backward_sum + column_of(shares[:, EXPERTS:], expert) * out
    half = Z * rows
    with jax.named_scope("cores"):
        others = [
            other_core(total[half:].astype(jnp.bfloat16)) for total in (forward_sum, backward_sum)
        ]
        mixture = forward_sum[:half] + others[0].astype(jnp.float32)
        back_mixture = backward_sum[:half] + others[1].astype(jnp.float32)
    with jax.named_scope("home"):
        passed = [total[half - rows :] for total in (mixture, back_mixture)]
        passed = along_z(jnp.concatenate(passed, axis=1).astype(jnp.bfloat16), -1)
        forward_next = send_home(mixture, tokens, passed[:, :model], 1)
        backward_next = send_home(back_mixture, upstream, passed[:, model:], -1)
    return (forward_next[None], backward_next[None])


def solution(mesh):
    by_token = P("pipe", "expert", None)
    return jax.shard_map(
        on_device,
        mesh=mesh,
        in_specs=(by_token,) * 3 + (P("pipe", None, "expert"),) + (by_token,) * 5,
        out_specs=(by_token, by_token),
        check_vma=False,
    )
```

```python
import jax
import jax.numpy as jnp
from jax import lax
from jax.sharding import PartitionSpec as P

EXPERTS = 4
Z = 4
CORES = 2
LANES = 128
CAP = 12


def expert_index(x, z, core):
    return (x * Z + z) * CORES + core


def expert_route(move):
    return [
        (expert_index(x, z, c), expert_index(*move(x, z, c)))
        for x in range(EXPERTS)
        for z in range(Z)
        for c in range(CORES)
    ]


def turn(core):
    return 1 - 2 * core


def along_z(block, distance):
    route = expert_route(lambda x, z, c: (x, (z + distance * turn(c)) % Z, c))
    return lax.ppermute(block, "expert", route)


def along_x(block, distance):
    route = expert_route(lambda x, z, c: ((x + distance * turn(c)) % EXPERTS, z, c))
    return lax.ppermute(block, "expert", route)


def other_core(block):
    return lax.ppermute(block, "expert", expert_route(lambda x, z, c: (x, z, 1 - c)))


def to_section(block, step, distance):
    sections = lax.axis_size("pipe")
    width = EXPERTS * Z * CORES
    route = [
        (p * width + source, (p + step) * width + target)
        for p in range(sections)
        if 0 <= p + step < sections
        for source, target in expert_route(lambda x, z, c: (x, (z + distance * turn(c)) % Z, c))
    ]
    return lax.ppermute(block, ("pipe", "expert"), route)


def together(*values):
    return lax.optimization_barrier(values)


def expert_hot(routes):
    return routes[:, :, None] == jnp.arange(EXPERTS, dtype=jnp.int32)


def expert_shares(hot, gates):
    return jnp.sum(jnp.where(hot, gates[:, :, None], 0.0), axis=1)


def expert_slots(hot):
    named = jnp.any(hot, axis=1)
    count = named.astype(jnp.int32)
    earlier = jnp.cumsum(count, axis=0) - count
    return jnp.where(named, earlier, -1).astype(jnp.float32)


def three_parts(values):
    first = lax.reduce_precision(values, 8, 7)
    second = lax.reduce_precision(values - first, 8, 7)
    return [part.astype(jnp.bfloat16) for part in (first, second, values - first - second)]


def side_columns(shares, slots):
    parts = jnp.concatenate(three_parts(shares) + [slots.astype(jnp.bfloat16)], axis=1)
    return jnp.pad(parts, ((0, 0), (0, LANES - parts.shape[1])))


def side_values(columns):
    width = 2 * EXPERTS
    parts = columns[:, : 4 * width].astype(jnp.float32)
    first, second, third, slots = jnp.split(parts, 4, axis=1)
    return first + second + third, slots


def column_of(table, index):
    hot = jnp.arange(table.shape[1], dtype=jnp.int32) == index
    return jnp.sum(jnp.where(hot[None, :], table, 0.0), axis=1, keepdims=True)


def placement(slots, expert, rows):
    slot = column_of(slots, expert)
    block = jnp.arange(slots.shape[0], dtype=jnp.int32) // rows
    place = jnp.arange(Z * CAP, dtype=jnp.int32)
    wanted = (place % CAP).astype(jnp.float32)
    found = (block[:, None] == place[None, :] // CAP) & (slot == wanted[None, :])
    return found.astype(jnp.bfloat16)


def dot(a, b):
    return jnp.dot(a, b, preferred_element_type=jnp.float32)


def dot_t(a, b):
    return lax.dot_general(a, b, (((1,), (1,)), ((), ())), preferred_element_type=jnp.float32)


def pack(places, block):
    packed = lax.dot_general(
        places,
        block,
        (((0,), (0,)), ((), ())),
        preferred_element_type=jnp.float32,
    )
    return packed.astype(jnp.bfloat16)


def forward_rows(rows, weight):
    width = 2 * weight.shape[1] // 3
    gate_val, up_val = jnp.split(dot(rows, weight[:, :width]), 2, axis=1)
    hidden = (jax.nn.silu(gate_val) * up_val).astype(jnp.bfloat16)
    return dot_t(hidden, weight[:, width:])


def backward_rows(rows, grads, weight):
    width = 2 * weight.shape[1] // 3
    hidden_grad = dot(grads, weight[:, width:])
    gate_val, up_val = jnp.split(dot(rows, weight[:, :width]), 2, axis=1)
    sig = jax.nn.sigmoid(gate_val)
    gate_grad = hidden_grad * up_val * sig * (1.0 + gate_val * (1.0 - sig))
    up_grad = hidden_grad * gate_val * sig
    grad = jnp.concatenate([gate_grad, up_grad], axis=1).astype(jnp.bfloat16)
    return dot_t(grad, weight[:, :width])


def pass_on(mixture):
    return along_z(jnp.split(mixture, Z, axis=0)[3].astype(jnp.bfloat16), -1)


def send_home(mixture, residual, passed, step):
    own, near, far = jnp.split(mixture, Z, axis=0)[:3]
    near = near + passed.astype(jnp.float32)
    total = to_section(own + residual.astype(jnp.float32), step, 0)
    total = total + to_section(far.astype(jnp.bfloat16), step, 1).astype(jnp.float32)
    total = total + to_section(near.astype(jnp.bfloat16), step, -1).astype(jnp.float32)
    return total.astype(jnp.bfloat16)


def on_device(
    forward_input,
    backward_input,
    backward_grad,
    gate_up_weight,
    down_weight,
    forward_routes,
    backward_routes,
    forward_gates,
    backward_gates,
):
    tokens, saved, upstream = forward_input[0], backward_input[0], backward_grad[0]
    rows, model = tokens.shape
    index = lax.axis_index("expert")
    turned = 1 - 2 * (index % CORES)
    me = index // (Z * CORES)
    experts = [(me + EXPERTS + d * turned) % EXPERTS for d in (0, -1, 1)]
    opposite = (me + 2) % EXPERTS
    half = Z * rows

    with jax.named_scope("gather_weights"):
        weights = jnp.concatenate([gate_up_weight[0], down_weight[0].T], axis=1)
        near, far = along_x(weights, 1), along_x(weights, -1)
        twin = other_core(weights)
    with jax.named_scope("forward_z"):
        hots = [expert_hot(forward_routes[0]), expert_hot(backward_routes[0])]
        shares = [
            expert_shares(hots[0], forward_gates[0]),
            expert_shares(hots[1], backward_gates[0]),
        ]
        slots = [expert_slots(hot) for hot in hots]
        side = side_columns(jnp.concatenate(shares, axis=1), jnp.concatenate(slots, axis=1))
        mine = jnp.concatenate([tokens, side], axis=1)
        below, above = along_z(mine, 1), along_z(mine, -1)
        back_mine = jnp.concatenate([saved, upstream], axis=1)
        below, above, twin, back_mine = together(below, above, twin, back_mine)
        mine = jnp.concatenate([mine, below, above, along_z(below, 1)], axis=0)
    with jax.named_scope("backward_z"):
        below, above = along_z(back_mine, 1), along_z(back_mine, -1)
        back_mine = jnp.concatenate([back_mine, below, above, along_z(below, 1)], axis=0)
    with jax.named_scope("forward_opposite"):
        block = mine[:, :model]
        shares, slots = side_values(mine[:, model:])
        place = placement(slots[:, :EXPERTS], opposite, rows)
        back_place = placement(slots[:, EXPERTS:], opposite, rows)
        visitors = along_x(pack(place, block), 2)
        mine, visitors = together(mine, visitors)
        out = sum(forward_rows(visitors, weight) for weight in (weights, twin))
        returned = along_x(out.astype(jnp.bfloat16), 2)
        near, far, returned = together(near, far, returned)
    with jax.named_scope("backward_opposite"):
        back_visitors = along_x(pack(back_place, back_mine), 2)
    with jax.named_scope("forward_experts"):
        other = other_core(mine)
        token_rows = jnp.concatenate([block, other[:, :model]], axis=0)
        other_shares, _ = side_values(other[:, model:])
        both_shares = jnp.concatenate([shares, other_shares], axis=0)
        total = 0.0
        for expert, weight in zip(experts, (weights, near, far)):
            share = column_of(both_shares[:, :EXPERTS], expert)
            total = total + share * forward_rows(token_rows, weight)
        swapped = other_core(total[half:].astype(jnp.bfloat16)).astype(jnp.float32)
        share = column_of(shares[:, :EXPERTS], opposite)
        mixture = total[:half] + swapped + share * dot(place, returned)
        forward_mixture, passed = mixture, pass_on(mixture)
    with jax.named_scope("backward_visitors"):
        out = sum(
            backward_rows(back_visitors[:, :model], back_visitors[:, model:], weight)
            for weight in (weights, twin)
        )
        back_returned = along_x(out.astype(jnp.bfloat16), 2)
    with jax.named_scope("backward_experts"):
        back_rows = jnp.concatenate([back_mine, other_core(back_mine)], axis=0)
        last, back_returned, passed = together(far, back_returned, passed)
        total = 0.0
        for expert, weight in zip(experts, (weights, near, last)):
            share = column_of(both_shares[:, EXPERTS:], expert)
            out = backward_rows(back_rows[:, :model], back_rows[:, model:], weight)
            total = total + share * out
        swapped = other_core(total[half:].astype(jnp.bfloat16)).astype(jnp.float32)
        share = column_of(shares[:, EXPERTS:], opposite)
        mixture = total[:half] + swapped + share * dot(back_place, back_returned)
    with jax.named_scope("forward_home"):
        forward_next = send_home(forward_mixture, tokens, passed, 1)
    with jax.named_scope("backward_home"):
        backward_next = send_home(mixture, upstream, pass_on(mixture), -1)
    return (forward_next[None], backward_next[None])


def solution(mesh):
    by_token = P("pipe", "expert", None)
    return jax.shard_map(
        on_device,
        mesh=mesh,
        in_specs=(by_token,) * 3 + (P("pipe", None, "expert"),) + (by_token,) * 5,
        out_specs=(by_token, by_token),
        check_vma=False,
    )
```

```python
import jax
import jax.numpy as jnp
from jax import lax
from jax.sharding import PartitionSpec as P

EXPERTS = 4
Z = 4
CORES = 2
LANES = 128


def expert_index(x, z, core):
    return (x * Z + z) * CORES + core


def expert_route(move):
    return [
        (expert_index(x, z, c), expert_index(*move(x, z, c)))
        for x in range(EXPERTS)
        for z in range(Z)
        for c in range(CORES)
    ]


def turn(core):
    return 1 - 2 * core


def along_z(block, distance):
    route = expert_route(lambda x, z, c: (x, (z + distance * turn(c)) % Z, c))
    return lax.ppermute(block, "expert", route)


def along_x(block, distance):
    route = expert_route(lambda x, z, c: ((x + distance * turn(c)) % EXPERTS, z, c))
    return lax.ppermute(block, "expert", route)


def other_core(block):
    return lax.ppermute(block, "expert", expert_route(lambda x, z, c: (x, z, 1 - c)))


def to_section(block, step):
    sections = lax.axis_size("pipe")
    route = [(p, p + step) for p in range(sections) if 0 <= p + step < sections]
    return lax.ppermute(block, "pipe", route)


def together(*values):
    return lax.optimization_barrier(values)


def expert_hot(routes):
    return routes[:, :, None] == jnp.arange(EXPERTS, dtype=jnp.int32)


def expert_shares(hot, gates):
    return jnp.sum(jnp.where(hot, gates[:, :, None], 0.0), axis=1)


def three_parts(values):
    first = lax.reduce_precision(values, 8, 7)
    second = lax.reduce_precision(values - first, 8, 7)
    return [part.astype(jnp.bfloat16) for part in (first, second, values - first - second)]


def side_columns(shares):
    parts = jnp.concatenate(three_parts(shares), axis=1)
    return jnp.pad(parts, ((0, 0), (0, LANES - parts.shape[1])))


def side_values(columns):
    width = 2 * EXPERTS
    first, second, third = jnp.split(columns[:, : 3 * width].astype(jnp.float32), 3, axis=1)
    return first + second + third


def column_of(table, index):
    hot = jnp.arange(table.shape[1], dtype=jnp.int32) == index
    return jnp.sum(jnp.where(hot[None, :], table, 0.0), axis=1, keepdims=True)


def dot(a, b):
    return jnp.dot(a, b, preferred_element_type=jnp.float32)


def dot_t(a, b):
    return lax.dot_general(a, b, (((1,), (1,)), ((), ())), preferred_element_type=jnp.float32)


def forward_rows(rows, gate_up, down):
    gate_val, up_val = jnp.split(dot(rows, gate_up), 2, axis=1)
    hidden = (jax.nn.silu(gate_val) * up_val).astype(jnp.bfloat16)
    return dot_t(hidden, down)


def backward_rows(rows, grads, gate_up, down):
    hidden_grad = dot(grads, down)
    gate_val, up_val = jnp.split(dot(rows, gate_up), 2, axis=1)
    sig = jax.nn.sigmoid(gate_val)
    gate_grad = hidden_grad * up_val * sig * (1.0 + gate_val * (1.0 - sig))
    up_grad = hidden_grad * gate_val * sig
    grad = jnp.concatenate([gate_grad, up_grad], axis=1).astype(jnp.bfloat16)
    return dot_t(grad, gate_up)


def on_device(
    forward_input,
    backward_input,
    backward_grad,
    gate_up_weight,
    down_weight,
    forward_routes,
    backward_routes,
    forward_gates,
    backward_gates,
):
    tokens, saved, upstream = forward_input[0], backward_input[0], backward_grad[0]
    rows, model = tokens.shape
    index = lax.axis_index("expert")
    turned = 1 - 2 * (index % CORES)
    me = index // (Z * CORES)
    experts = [(me + EXPERTS + d * turned) % EXPERTS for d in (0, -1, 1, -2)]

    with jax.named_scope("gather_weights"):
        weights = jnp.concatenate([gate_up_weight[0], down_weight[0].T], axis=1)
        near, far = along_x(weights, 1), along_x(weights, -1)
    with jax.named_scope("gather_rows"):
        shares = [
            expert_shares(expert_hot(forward_routes[0]), forward_gates[0]),
            expert_shares(expert_hot(backward_routes[0]), backward_gates[0]),
        ]
        side = side_columns(jnp.concatenate(shares, axis=1))
        mine = jnp.concatenate([tokens, saved, upstream, side], axis=1)
        below, above = along_z(mine, 1), along_z(mine, -1)
        opposite = along_z(below, 1)
    with jax.named_scope("gather_opposite"):
        near, far, below, above, opposite = together(near, far, below, above, opposite)
        weights = [weights, near, far, along_x(near, 1)]
        mine = jnp.concatenate([mine, below, above, opposite], axis=0)
        both = [mine, other_core(mine)]
        cuts = (0, model, 2 * model, 3 * model, 3 * model + LANES)
        token_rows, saved_rows, upstream_rows, sides = [
            jnp.concatenate([part[:, low:high] for part in both], axis=0)
            for low, high in zip(cuts, cuts[1:])
        ]
        shares = side_values(sides)
    with jax.named_scope("experts"):
        forward_sum = backward_sum = 0.0
        width = gate_up_weight.shape[2]
        for expert, weight in zip(experts, weights):
            gate_up, down = weight[:, :width], weight[:, width:]
            out = forward_rows(token_rows, gate_up, down)
            forward_sum = forward_sum + column_of(shares[:, :EXPERTS], expert) * out
            out = backward_rows(saved_rows, upstream_rows, gate_up, down)
            backward_sum = backward_sum + column_of(shares[:, EXPERTS:], expert) * out
    half = Z * rows
    with jax.named_scope("cores"):
        total = jnp.concatenate([forward_sum, backward_sum], axis=1)
        other = other_core(total[half:].astype(jnp.bfloat16))
        total = total[:half] + other.astype(jnp.float32)
    with jax.named_scope("home"):
        own, near, far, passed = jnp.split(total, Z, axis=0)
        passed = along_z(passed.astype(jnp.bfloat16), -1)
        far = along_z(far.astype(jnp.bfloat16), 1)
        near = along_z((near + passed.astype(jnp.float32)).astype(jnp.bfloat16), -1)
        residual = jnp.concatenate([tokens, upstream], axis=1).astype(jnp.float32)
        total = own + residual + far.astype(jnp.float32) + near.astype(jnp.float32)
        total = total.astype(jnp.bfloat16)
    with jax.named_scope("sections"):
        forward_next = to_section(total[:, :model], 1)
        backward_next = to_section(total[:, model:], -1)
    return (forward_next[None], backward_next[None])


def solution(mesh):
    by_token = P("pipe", "expert", None)
    return jax.shard_map(
        on_device,
        mesh=mesh,
        in_specs=(by_token,) * 3 + (P("pipe", None, "expert"),) + (by_token,) * 5,
        out_specs=(by_token, by_token),
        check_vma=False,
    )
```

```python
import jax
import jax.numpy as jnp
from jax import lax
from jax.experimental import pallas as pl
from jax.experimental.pallas import tpu as pltpu
from jax.sharding import PartitionSpec as P

EXPERTS = 4
Z = 4
CORES = 2
LANES = 128
CHUNK = 512
ROOM = 40 * 1024 * 1024


def expert_index(x, z, core):
    return (x * Z + z) * CORES + core


def expert_route(move):
    return [
        (expert_index(x, z, c), expert_index(*move(x, z, c)))
        for x in range(EXPERTS)
        for z in range(Z)
        for c in range(CORES)
    ]


def turn(core):
    return 1 - 2 * core


def along_z(block, distance):
    route = expert_route(lambda x, z, c: (x, (z + distance * turn(c)) % Z, c))
    return lax.ppermute(block, "expert", route)


def along_x(block, distance):
    route = expert_route(lambda x, z, c: ((x + distance * turn(c)) % EXPERTS, z, c))
    return lax.ppermute(block, "expert", route)


def other_core(block):
    return lax.ppermute(block, "expert", expert_route(lambda x, z, c: (x, z, 1 - c)))


def to_section(block, step):
    sections = lax.axis_size("pipe")
    route = [(p, p + step) for p in range(sections) if 0 <= p + step < sections]
    return lax.ppermute(block, "pipe", route)


def together(*values):
    return lax.optimization_barrier(values)


def expert_hot(routes):
    return routes[:, :, None] == jnp.arange(EXPERTS, dtype=jnp.int32)


def expert_shares(hot, gates):
    return jnp.sum(jnp.where(hot, gates[:, :, None], 0.0), axis=1)


def three_parts(values):
    first = lax.reduce_precision(values, 8, 7)
    second = lax.reduce_precision(values - first, 8, 7)
    return [part.astype(jnp.bfloat16) for part in (first, second, values - first - second)]


def side_columns(shares):
    parts = jnp.concatenate(three_parts(shares), axis=1)
    return jnp.pad(parts, ((0, 0), (0, LANES - parts.shape[1])))


def share_picks(experts):
    lane = jnp.arange(LANES, dtype=jnp.int32)
    wanted = jnp.stack(experts + [EXPERTS + e for e in experts])
    picks = (lane[:, None] % (2 * EXPERTS) == wanted[None, :]) & (lane[:, None] < 6 * EXPERTS)
    return jnp.pad(picks.astype(jnp.bfloat16), ((0, 0), (0, LANES - wanted.shape[0])))


def dot(a, b):
    return jnp.dot(a, b, preferred_element_type=jnp.float32)


def dot_t(a, b):
    return lax.dot_general(a, b, (((1,), (1,)), ((), ())), preferred_element_type=jnp.float32)


def fill_rows(mine, other, rows):
    half, model = mine.shape[0], rows[0].shape[1]
    for k, target in enumerate(rows):
        target[:half, :] = mine[:, k * model : (k + 1) * model]
        target[half:, :] = other[:, k * model : (k + 1) * model]


def pick_shares(mine, other, picks, model):
    sides = [part[:, 3 * model :] for part in (mine, other)]
    return jnp.concatenate([dot(side, picks[...]) for side in sides], axis=0)


def one_expert(rows, weight, share, back_share):
    token, saved, upstream = rows
    half = weight.shape[1] // 3
    both = dot(token[...], weight[:, : 2 * half])
    gate_val, up_val = both[:, :half], both[:, half:]
    hidden = (gate_val * jax.nn.sigmoid(gate_val) * up_val).astype(jnp.bfloat16)
    hidden_grad = dot(upstream[...], weight[:, 2 * half :])
    both = dot(saved[...], weight[:, : 2 * half])
    gate_val, up_val = both[:, :half], both[:, half:]
    sig = jax.nn.sigmoid(gate_val)
    gate_grad = hidden_grad * up_val * sig * (1.0 + gate_val * (1.0 - sig))
    up_grad = hidden_grad * gate_val * sig
    grad = jnp.concatenate([gate_grad, up_grad], axis=1).astype(jnp.bfloat16)
    for low in range(0, token.shape[1], CHUNK):
        cut = slice(low, low + CHUNK)
        out = share * dot_t(hidden, weight[cut, 2 * half :])
        yield cut, out, back_share * dot_t(grad, weight[cut, : 2 * half])


def first_kernel(mine, other, picks, *refs):
    weights, (total, back_total), rows = refs[:3], refs[3:5], refs[5:]
    fill_rows(mine, other, rows)
    shares = pick_shares(mine, other, picks, rows[0].shape[1])
    for k, weight in enumerate(weights):
        share, back_share = shares[:, k : k + 1], shares[:, 3 + k : 4 + k]
        for cut, out, back_out in one_expert(rows, weight, share, back_share):
            if k > 0:
                out, back_out = out + total[:, cut], back_out + back_total[:, cut]
            total[:, cut], back_total[:, cut] = out, back_out


def last_kernel(mine, other, picks, weight, total, back_total, keep, give, *rows):
    fill_rows(mine, other, rows)
    half, model = mine.shape[0], rows[0].shape[1]
    shares = pick_shares(mine, other, picks, model)
    for cut, out, back_out in one_expert(rows, weight, shares[:, :1], shares[:, 1:2]):
        back_cut = slice(model + cut.start, model + cut.stop)
        out, back_out = out + total[:, cut], back_out + back_total[:, cut]
        keep[:, cut], keep[:, back_cut] = out[:half], back_out[:half]
        give[:, cut] = out[half:].astype(jnp.bfloat16)
        give[:, back_cut] = back_out[half:].astype(jnp.bfloat16)


def run_kernel(kernel, operands, outs, model):
    whole = pl.BlockSpec(memory_space=pltpu.VMEM)
    both = 2 * operands[0].shape[0]
    return pl.pallas_call(
        kernel,
        out_shape=outs,
        in_specs=[whole] * len(operands),
        out_specs=tuple(whole for _ in outs),
        scratch_shapes=[pltpu.VMEM((both, model), jnp.bfloat16) for _ in range(3)],
        compiler_params=pltpu.CompilerParams(vmem_limit_bytes=ROOM),
        cost_estimate=pl.CostEstimate(flops=1000, bytes_accessed=1000, transcendentals=0),
    )(*operands)


def on_device(
    forward_input,
    backward_input,
    backward_grad,
    gate_up_weight,
    down_weight,
    forward_routes,
    backward_routes,
    forward_gates,
    backward_gates,
):
    tokens, saved, upstream = forward_input[0], backward_input[0], backward_grad[0]
    rows, model = tokens.shape
    index = lax.axis_index("expert")
    turned = 1 - 2 * (index % CORES)
    me = index // (Z * CORES)
    experts = [(me + EXPERTS + d * turned) % EXPERTS for d in (0, -1, 1, -2)]

    with jax.named_scope("gather_weights"):
        weights = jnp.concatenate([gate_up_weight[0], down_weight[0].T], axis=1)
        near, far = along_x(weights, 1), along_x(weights, -1)
    with jax.named_scope("gather_rows"):
        shares = [
            expert_shares(expert_hot(forward_routes[0]), forward_gates[0]),
            expert_shares(expert_hot(backward_routes[0]), backward_gates[0]),
        ]
        side = side_columns(jnp.concatenate(shares, axis=1))
        mine = jnp.concatenate([tokens, saved, upstream, side], axis=1)
        below, above = along_z(mine, 1), along_z(mine, -1)
        opposite = along_z(below, 1)
    with jax.named_scope("gather_opposite"):
        near, far, below, above, opposite = together(near, far, below, above, opposite)
        weights = [weights, near, far, along_x(near, 1)]
        mine = jnp.concatenate([mine, below, above, opposite], axis=0)
        other = other_core(mine)
    half = Z * rows
    with jax.named_scope("experts"):
        outs = (jax.ShapeDtypeStruct((2 * half, model), jnp.float32),) * 2
        operands = (mine, other, share_picks(experts[:3]), *weights[:3])
        sums = run_kernel(first_kernel, operands, outs, model)
    with jax.named_scope("last_expert"):
        outs = (
            jax.ShapeDtypeStruct((half, 2 * model), jnp.float32),
            jax.ShapeDtypeStruct((half, 2 * model), jnp.bfloat16),
        )
        operands = (mine, other, share_picks(experts[3:]), weights[3], *sums)
        keep, give = run_kernel(last_kernel, operands, outs, model)
    with jax.named_scope("cores"):
        total = keep + other_core(give).astype(jnp.float32)
    with jax.named_scope("home"):
        own, near, far, passed = jnp.split(total, Z, axis=0)
        passed = along_z(passed.astype(jnp.bfloat16), -1)
        far = along_z(far.astype(jnp.bfloat16), 1)
        near = along_z((near + passed.astype(jnp.float32)).astype(jnp.bfloat16), -1)
        residual = jnp.concatenate([tokens, upstream], axis=1).astype(jnp.float32)
        total = own + residual + far.astype(jnp.float32) + near.astype(jnp.float32)
        total = total.astype(jnp.bfloat16)
    with jax.named_scope("sections"):
        forward_next = to_section(total[:, :model], 1)
        backward_next = to_section(total[:, model:], -1)
    return (forward_next[None], backward_next[None])


def solution(mesh):
    by_token = P("pipe", "expert", None)
    return jax.shard_map(
        on_device,
        mesh=mesh,
        in_specs=(by_token,) * 3 + (P("pipe", None, "expert"),) + (by_token,) * 5,
        out_specs=(by_token, by_token),
        check_vma=False,
    )
```

```python
import jax
import jax.numpy as jnp
from jax import lax
from jax.experimental import pallas as pl
from jax.experimental.pallas import tpu as pltpu
from jax.sharding import PartitionSpec as P

EXPERTS = 4
Z = 4
CORES = 2
LANES = 128
CHUNK = 256
JOIN_PIECES = 4
ROOM = 40 * 1024 * 1024


def expert_index(x, z, core):
    return (x * Z + z) * CORES + core


def expert_route(move):
    return [
        (expert_index(x, z, c), expert_index(*move(x, z, c)))
        for x in range(EXPERTS)
        for z in range(Z)
        for c in range(CORES)
    ]


def turn(core):
    return 1 - 2 * core


def along_z(block, distance):
    route = expert_route(lambda x, z, c: (x, (z + distance * turn(c)) % Z, c))
    return lax.ppermute(block, "expert", route)


def along_x(block, distance):
    route = expert_route(lambda x, z, c: ((x + distance * turn(c)) % EXPERTS, z, c))
    return lax.ppermute(block, "expert", route)


def other_core(block):
    return lax.ppermute(block, "expert", expert_route(lambda x, z, c: (x, z, 1 - c)))


def to_section(block, step, distance):
    sections = lax.axis_size("pipe")
    width = EXPERTS * Z * CORES
    route = [
        (p * width + source, (p + step) * width + target)
        for p in range(sections)
        if 0 <= p + step < sections
        for source, target in expert_route(lambda x, z, c: (x, (z + distance * turn(c)) % Z, c))
    ]
    return lax.ppermute(block, ("pipe", "expert"), route)


def together(*values):
    return lax.optimization_barrier(values)


def expert_hot(routes):
    return routes[:, :, None] == jnp.arange(EXPERTS, dtype=jnp.int32)


def expert_shares(hot, gates):
    return jnp.sum(jnp.where(hot, gates[:, :, None], 0.0), axis=1)


def three_parts(values):
    first = lax.reduce_precision(values, 8, 7)
    second = lax.reduce_precision(values - first, 8, 7)
    return [part.astype(jnp.bfloat16) for part in (first, second, values - first - second)]


def side_columns(shares):
    parts = jnp.concatenate(three_parts(shares), axis=1)
    return jnp.pad(parts, ((0, 0), (0, LANES - parts.shape[1])))


def share_picks(experts):
    lane = jnp.arange(LANES, dtype=jnp.int32)
    wanted = jnp.stack(experts + [EXPERTS + e for e in experts])
    picks = (lane[:, None] % (2 * EXPERTS) == wanted[None, :]) & (lane[:, None] < 6 * EXPERTS)
    return jnp.pad(picks.astype(jnp.bfloat16), ((0, 0), (0, LANES - wanted.shape[0])))


def dot(a, b):
    return jnp.dot(a, b, preferred_element_type=jnp.float32)


def dot_t(a, b):
    return lax.dot_general(a, b, (((1,), (1,)), ((), ())), preferred_element_type=jnp.float32)


def join_kernel(gate_up, down, joined, done):
    model, depth = gate_up.shape[0], down.shape[0]
    piece = model // JOIN_PIECES
    pairs = [
        (gate_up.at[pl.ds(k * piece, piece), :], joined.at[pl.ds(k * piece, piece), :])
        for k in range(JOIN_PIECES)
    ]
    pairs += [
        (down.at[:, pl.ds(k * CHUNK, CHUNK)], joined.at[pl.ds(model + k * depth, depth), :])
        for k in range(model // CHUNK)
    ]
    copies = [
        pltpu.make_async_copy(source, target, done.at[k])
        for k, (source, target) in enumerate(pairs)
    ]
    for copy in copies:
        copy.start()
    for copy in copies:
        copy.wait()


def join_weights(gate_up, down):
    model, depth = gate_up.shape[0], down.shape[0]
    anywhere = pl.BlockSpec(memory_space=pl.ANY)
    rows = model + model // CHUNK * depth
    return pl.pallas_call(
        join_kernel,
        out_shape=jax.ShapeDtypeStruct((rows, CHUNK), gate_up.dtype),
        in_specs=[anywhere, anywhere],
        out_specs=anywhere,
        scratch_shapes=[pltpu.SemaphoreType.DMA((JOIN_PIECES + model // CHUNK,))],
    )(gate_up, down)


def fill_rows(mine, other, rows):
    half, model = mine.shape[0], rows[0].shape[1]
    for k, target in enumerate(rows):
        target[:half, :] = mine[:, k * model : (k + 1) * model]
        target[half:, :] = other[:, k * model : (k + 1) * model]


def pick_shares(mine, other, picks, model):
    sides = [part[:, 3 * model :] for part in (mine, other)]
    return jnp.concatenate([dot(side, picks[...]) for side in sides], axis=0)


def one_expert(rows, weight, share, back_share):
    token, saved, upstream = rows
    model, half = token.shape[1], CHUNK // 2
    cuts = [slice(low, low + CHUNK) for low in range(0, model, CHUNK)]
    downs = [slice(model + k * half, model + (k + 1) * half) for k in range(len(cuts))]
    gate_up = weight[:model, :]
    both = dot(token[...], gate_up)
    gate_val, up_val = both[:, :half], both[:, half:]
    hidden = (gate_val * jax.nn.sigmoid(gate_val) * up_val).astype(jnp.bfloat16)
    hidden_grad = sum(dot_t(upstream[:, cut], weight[at, :]) for cut, at in zip(cuts, downs))
    both = dot(saved[...], gate_up)
    gate_val, up_val = both[:, :half], both[:, half:]
    sig = jax.nn.sigmoid(gate_val)
    gate_grad = hidden_grad * up_val * sig * (1.0 + gate_val * (1.0 - sig))
    up_grad = hidden_grad * gate_val * sig
    grad = jnp.concatenate([gate_grad, up_grad], axis=1).astype(jnp.bfloat16)
    for cut, at in zip(cuts, downs):
        yield cut, share * dot(hidden, weight[at, :]), back_share * dot_t(grad, weight[cut, :])


def first_kernel(mine, other, picks, *refs):
    weights, (total, back_total), rows, shares = refs[:3], refs[3:5], refs[5:8], refs[8]
    fill_rows(mine, other, rows)
    shares[...] = pick_shares(mine, other, picks, rows[0].shape[1])
    for k, weight in enumerate(weights):
        share, back_share = shares[:, k : k + 1], shares[:, EXPERTS + k : EXPERTS + k + 1]
        for cut, out, back_out in one_expert(rows, weight, share, back_share):
            if k > 0:
                out, back_out = out + total[:, cut], back_out + back_total[:, cut]
            total[:, cut], back_total[:, cut] = out, back_out


def last_kernel(total, back_total, token, saved, upstream, shares, weight, keep, give):
    half, model = keep.shape[0], token.shape[1]
    share, back_share = shares[:, EXPERTS - 1 : EXPERTS], shares[:, 2 * EXPERTS - 1 : 2 * EXPERTS]
    for cut, out, back_out in one_expert((token, saved, upstream), weight, share, back_share):
        back_cut = slice(model + cut.start, model + cut.stop)
        out, back_out = out + total[:, cut], back_out + back_total[:, cut]
        keep[:, cut], keep[:, back_cut] = out[:half], back_out[:half]
        give[:, cut] = out[half:].astype(jnp.bfloat16)
        give[:, back_cut] = back_out[half:].astype(jnp.bfloat16)


def run_kernel(kernel, operands, outs):
    whole = pl.BlockSpec(memory_space=pltpu.VMEM)
    return pl.pallas_call(
        kernel,
        out_shape=outs,
        in_specs=[whole] * len(operands),
        out_specs=tuple(whole for _ in outs),
        compiler_params=pltpu.CompilerParams(vmem_limit_bytes=ROOM),
        cost_estimate=pl.CostEstimate(flops=1000, bytes_accessed=1000, transcendentals=0),
    )(*operands)


def on_device(
    forward_input,
    backward_input,
    backward_grad,
    gate_up_weight,
    down_weight,
    forward_routes,
    backward_routes,
    forward_gates,
    backward_gates,
):
    tokens, saved, upstream = forward_input[0], backward_input[0], backward_grad[0]
    rows, model = tokens.shape
    index = lax.axis_index("expert")
    turned = 1 - 2 * (index % CORES)
    me = index // (Z * CORES)
    experts = [(me + EXPERTS + d * turned) % EXPERTS for d in (0, -1, 1, -2)]

    with jax.named_scope("gather_weights"):
        weights = join_weights(gate_up_weight[0], down_weight[0])
        near, far = along_x(weights, 1), along_x(weights, -1)
    with jax.named_scope("gather_rows"):
        shares = [
            expert_shares(expert_hot(forward_routes[0]), forward_gates[0]),
            expert_shares(expert_hot(backward_routes[0]), backward_gates[0]),
        ]
        side = side_columns(jnp.concatenate(shares, axis=1))
        mine = jnp.concatenate([tokens, saved, upstream, side], axis=1)
        below, above = along_z(mine, 1), along_z(mine, -1)
        opposite = along_z(below, 1)
    with jax.named_scope("gather_opposite"):
        near, far, below, above, opposite = together(near, far, below, above, opposite)
        weights = [weights, near, far, along_x(near, 1)]
        mine = jnp.concatenate([mine, below, above, opposite], axis=0)
        other = other_core(mine)
    half = Z * rows
    with jax.named_scope("experts"):
        outs = [jax.ShapeDtypeStruct((2 * half, model), jnp.float32)] * 2
        outs += [jax.ShapeDtypeStruct((2 * half, model), jnp.bfloat16)] * 3
        outs += [jax.ShapeDtypeStruct((2 * half, LANES), jnp.float32)]
        sums = run_kernel(first_kernel, (mine, other, share_picks(experts), *weights[:3]), outs)
    with jax.named_scope("residual"):
        tokens, upstream, *sums = together(tokens, upstream, *sums)
        residuals = to_section(tokens, 1, 0), to_section(upstream, -1, 0)
        *residuals, last_weight = together(*residuals, weights[3])
    with jax.named_scope("last_expert"):
        outs = (
            jax.ShapeDtypeStruct((half, 2 * model), jnp.float32),
            jax.ShapeDtypeStruct((half, 2 * model), jnp.bfloat16),
        )
        keep, give = run_kernel(last_kernel, (*sums, last_weight), outs)
    with jax.named_scope("cores"):
        total = keep + other_core(give).astype(jnp.float32)
    with jax.named_scope("home"):
        own, near, far, passed = jnp.split(total, Z, axis=0)
        passed = along_z(passed.astype(jnp.bfloat16), -1)
        own, far = own.astype(jnp.bfloat16), far.astype(jnp.bfloat16)
        parts = [to_section(own[:, :model], 1, 0), to_section(own[:, model:], -1, 0)]
        parts += [to_section(far[:, :model], 1, 1), to_section(far[:, model:], -1, 1)]
        passed, *parts = together(passed, *parts)
        near = (near + passed.astype(jnp.float32)).astype(jnp.bfloat16)
        parts += [to_section(near[:, :model], 1, -1), to_section(near[:, model:], -1, -1)]
        sides = [[residuals[k]] + parts[k::2] for k in range(2)]
        forward_next, backward_next = [
            sum(part.astype(jnp.float32) for part in side).astype(jnp.bfloat16) for side in sides
        ]
    return (forward_next[None], backward_next[None])


def solution(mesh):
    by_token = P("pipe", "expert", None)
    return jax.shard_map(
        on_device,
        mesh=mesh,
        in_specs=(by_token,) * 3 + (P("pipe", None, "expert"),) + (by_token,) * 5,
        out_specs=(by_token, by_token),
        check_vma=False,
    )
```

```python
import jax
import jax.numpy as jnp
from jax import lax
from jax.experimental import pallas as pl
from jax.experimental.pallas import tpu as pltpu
from jax.sharding import PartitionSpec as P

EXPERTS = 4
Z = 4
CORES = 2
LANES = 128
CHUNK = 256
JOIN_PIECES = 4
ROOM = 40 * 1024 * 1024


def expert_index(x, z, core):
    return (x * Z + z) * CORES + core


def expert_route(move):
    return [
        (expert_index(x, z, c), expert_index(*move(x, z, c)))
        for x in range(EXPERTS)
        for z in range(Z)
        for c in range(CORES)
    ]


def turn(core):
    return 1 - 2 * core


def along_z(block, distance):
    route = expert_route(lambda x, z, c: (x, (z + distance * turn(c)) % Z, c))
    return lax.ppermute(block, "expert", route)


def along_x(block, distance):
    route = expert_route(lambda x, z, c: ((x + distance * turn(c)) % EXPERTS, z, c))
    return lax.ppermute(block, "expert", route)


def other_core(block):
    return lax.ppermute(block, "expert", expert_route(lambda x, z, c: (x, z, 1 - c)))


def to_section(block, step, distance):
    sections = lax.axis_size("pipe")
    width = EXPERTS * Z * CORES
    route = [
        (p * width + source, (p + step) * width + target)
        for p in range(sections)
        if 0 <= p + step < sections
        for source, target in expert_route(lambda x, z, c: (x, (z + distance * turn(c)) % Z, c))
    ]
    return lax.ppermute(block, ("pipe", "expert"), route)


def together(*values):
    return lax.optimization_barrier(values)


def expert_hot(routes):
    return routes[:, :, None] == jnp.arange(EXPERTS, dtype=jnp.int32)


def expert_shares(hot, gates):
    return jnp.sum(jnp.where(hot, gates[:, :, None], 0.0), axis=1)


def three_parts(values):
    first = lax.reduce_precision(values, 8, 7)
    second = lax.reduce_precision(values - first, 8, 7)
    return [part.astype(jnp.bfloat16) for part in (first, second, values - first - second)]


def side_columns(shares):
    parts = jnp.concatenate(three_parts(shares), axis=1)
    return jnp.pad(parts, ((0, 0), (0, LANES - parts.shape[1])))


def share_picks(experts):
    lane = jnp.arange(LANES, dtype=jnp.int32)
    wanted = jnp.stack(experts + [EXPERTS + e for e in experts])
    picks = (lane[:, None] % (2 * EXPERTS) == wanted[None, :]) & (lane[:, None] < 6 * EXPERTS)
    return jnp.pad(picks.astype(jnp.bfloat16), ((0, 0), (0, LANES - wanted.shape[0])))


def dot(a, b):
    return jnp.dot(a, b, preferred_element_type=jnp.float32)


def dot_t(a, b):
    return lax.dot_general(a, b, (((1,), (1,)), ((), ())), preferred_element_type=jnp.float32)


def join_kernel(gate_up, down, joined, done):
    model, depth = gate_up.shape[0], down.shape[0]
    piece = model // JOIN_PIECES
    pairs = [
        (gate_up.at[pl.ds(k * piece, piece), :], joined.at[pl.ds(k * piece, piece), :])
        for k in range(JOIN_PIECES)
    ]
    pairs += [
        (down.at[:, pl.ds(k * CHUNK, CHUNK)], joined.at[pl.ds(model + k * depth, depth), :])
        for k in range(model // CHUNK)
    ]
    copies = [
        pltpu.make_async_copy(source, target, done.at[k])
        for k, (source, target) in enumerate(pairs)
    ]
    for copy in copies:
        copy.start()
    for copy in copies:
        copy.wait()


def join_weights(gate_up, down):
    model, depth = gate_up.shape[0], down.shape[0]
    anywhere = pl.BlockSpec(memory_space=pl.ANY)
    rows = model + model // CHUNK * depth
    return pl.pallas_call(
        join_kernel,
        out_shape=jax.ShapeDtypeStruct((rows, CHUNK), gate_up.dtype),
        in_specs=[anywhere, anywhere],
        out_specs=pl.BlockSpec(memory_space=pltpu.VMEM),
        scratch_shapes=[pltpu.SemaphoreType.DMA((JOIN_PIECES + model // CHUNK,))],
    )(gate_up, down)


def fill_rows(mine, other, rows):
    half, model = mine.shape[0], rows[0].shape[1]
    for k, target in enumerate(rows):
        target[:half, :] = mine[:, k * model : (k + 1) * model]
        target[half:, :] = other[:, k * model : (k + 1) * model]


def pick_shares(mine, other, picks, model):
    sides = [part[:, 3 * model :] for part in (mine, other)]
    return jnp.concatenate([dot(side, picks[...]) for side in sides], axis=0)


def one_expert(rows, weight, share, back_share):
    token, saved, upstream = rows
    model, half = token.shape[1], CHUNK // 2
    cuts = [slice(low, low + CHUNK) for low in range(0, model, CHUNK)]
    downs = [slice(model + k * half, model + (k + 1) * half) for k in range(len(cuts))]
    gate_up = weight[:model, :]
    both = dot(token[...], gate_up)
    gate_val, up_val = both[:, :half], both[:, half:]
    hidden = (gate_val * jax.nn.sigmoid(gate_val) * up_val).astype(jnp.bfloat16)
    hidden_grad = sum(dot_t(upstream[:, cut], weight[at, :]) for cut, at in zip(cuts, downs))
    both = dot(saved[...], gate_up)
    gate_val, up_val = both[:, :half], both[:, half:]
    sig = jax.nn.sigmoid(gate_val)
    gate_grad = hidden_grad * up_val * sig * (1.0 + gate_val * (1.0 - sig))
    up_grad = hidden_grad * gate_val * sig
    grad = jnp.concatenate([gate_grad, up_grad], axis=1).astype(jnp.bfloat16)
    for cut, at in zip(cuts, downs):
        yield cut, share * dot(hidden, weight[at, :]), back_share * dot_t(grad, weight[cut, :])


def first_kernel(mine, other, picks, *refs):
    weights, (total, back_total), rows, shares = refs[:3], refs[3:5], refs[5:8], refs[8]
    fill_rows(mine, other, rows)
    shares[...] = pick_shares(mine, other, picks, rows[0].shape[1])
    for k, weight in enumerate(weights):
        share, back_share = shares[:, k : k + 1], shares[:, EXPERTS + k : EXPERTS + k + 1]
        for cut, out, back_out in one_expert(rows, weight, share, back_share):
            if k > 0:
                out, back_out = out + total[:, cut], back_out + back_total[:, cut]
            total[:, cut], back_total[:, cut] = out, back_out


def last_kernel(total, back_total, token, saved, upstream, shares, weight, keep, give):
    half, model = keep.shape[0], token.shape[1]
    share, back_share = shares[:, EXPERTS - 1 : EXPERTS], shares[:, 2 * EXPERTS - 1 : 2 * EXPERTS]
    for cut, out, back_out in one_expert((token, saved, upstream), weight, share, back_share):
        back_cut = slice(model + cut.start, model + cut.stop)
        out, back_out = out + total[:, cut], back_out + back_total[:, cut]
        keep[:, cut], keep[:, back_cut] = out[:half], back_out[:half]
        give[:, cut] = out[half:].astype(jnp.bfloat16)
        give[:, back_cut] = back_out[half:].astype(jnp.bfloat16)


def run_kernel(kernel, operands, outs):
    whole = pl.BlockSpec(memory_space=pltpu.VMEM)
    return pl.pallas_call(
        kernel,
        out_shape=outs,
        in_specs=[whole] * len(operands),
        out_specs=tuple(whole for _ in outs),
        compiler_params=pltpu.CompilerParams(vmem_limit_bytes=ROOM),
        cost_estimate=pl.CostEstimate(flops=1000, bytes_accessed=1000, transcendentals=0),
    )(*operands)


def on_device(
    forward_input,
    backward_input,
    backward_grad,
    gate_up_weight,
    down_weight,
    forward_routes,
    backward_routes,
    forward_gates,
    backward_gates,
):
    tokens, saved, upstream = forward_input[0], backward_input[0], backward_grad[0]
    rows, model = tokens.shape
    index = lax.axis_index("expert")
    turned = 1 - 2 * (index % CORES)
    me = index // (Z * CORES)
    experts = [(me + EXPERTS + d * turned) % EXPERTS for d in (0, -1, 1, -2)]

    with jax.named_scope("gather_weights"):
        weights = join_weights(gate_up_weight[0], down_weight[0])
        near, far = along_x(weights, 1), along_x(weights, -1)
    with jax.named_scope("gather_rows"):
        shares = [
            expert_shares(expert_hot(forward_routes[0]), forward_gates[0]),
            expert_shares(expert_hot(backward_routes[0]), backward_gates[0]),
        ]
        side = side_columns(jnp.concatenate(shares, axis=1))
        mine = jnp.concatenate([tokens, saved, upstream, side], axis=1)
        below, above = along_z(mine, 1), along_z(mine, -1)
        opposite = along_z(below, 1)
    with jax.named_scope("gather_opposite"):
        near, far, below, above, opposite = together(near, far, below, above, opposite)
        weights = [weights, near, far, along_x(near, 1)]
        mine = jnp.concatenate([mine, below, above, opposite], axis=0)
        other = other_core(mine)
    half = Z * rows
    with jax.named_scope("experts"):
        outs = [jax.ShapeDtypeStruct((2 * half, model), jnp.float32)] * 2
        outs += [jax.ShapeDtypeStruct((2 * half, model), jnp.bfloat16)] * 3
        outs += [jax.ShapeDtypeStruct((2 * half, LANES), jnp.float32)]
        sums = run_kernel(first_kernel, (mine, other, share_picks(experts), *weights[:3]), outs)
    with jax.named_scope("residual"):
        tokens, upstream, *sums = together(tokens, upstream, *sums)
        residuals = to_section(tokens, 1, 0), to_section(upstream, -1, 0)
        *residuals, last_weight = together(*residuals, weights[3])
    with jax.named_scope("last_expert"):
        outs = (
            jax.ShapeDtypeStruct((half, 2 * model), jnp.float32),
            jax.ShapeDtypeStruct((half, 2 * model), jnp.bfloat16),
        )
        keep, give = run_kernel(last_kernel, (*sums, last_weight), outs)
    with jax.named_scope("cores"):
        total = keep + other_core(give).astype(jnp.float32)
    with jax.named_scope("home"):
        own, near, far, passed = jnp.split(total, Z, axis=0)
        passed = along_z(passed.astype(jnp.bfloat16), -1)
        own, far = own.astype(jnp.bfloat16), far.astype(jnp.bfloat16)
        parts = [to_section(own[:, :model], 1, 0), to_section(own[:, model:], -1, 0)]
        parts += [to_section(far[:, :model], 1, 1), to_section(far[:, model:], -1, 1)]
        passed, *parts = together(passed, *parts)
        near = (near + passed.astype(jnp.float32)).astype(jnp.bfloat16)
        parts += [to_section(near[:, :model], 1, -1), to_section(near[:, model:], -1, -1)]
        sides = [[residuals[k]] + parts[k::2] for k in range(2)]
        forward_next, backward_next = [
            sum(part.astype(jnp.float32) for part in side).astype(jnp.bfloat16) for side in sides
        ]
    return (forward_next[None], backward_next[None])


def solution(mesh):
    by_token = P("pipe", "expert", None)
    return jax.shard_map(
        on_device,
        mesh=mesh,
        in_specs=(by_token,) * 3 + (P("pipe", None, "expert"),) + (by_token,) * 5,
        out_specs=(by_token, by_token),
        check_vma=False,
    )
```

```python
import jax
import jax.numpy as jnp
from jax import lax
from jax.experimental import pallas as pl
from jax.experimental.pallas import tpu as pltpu
from jax.sharding import PartitionSpec as P

EXPERTS = 4
Z = 4
CORES = 2
LANES = 128
CHUNK = 256
JOIN_PIECES = 4
ROOM = 40 * 1024 * 1024


def expert_index(x, z, core):
    return (x * Z + z) * CORES + core


def expert_route(move):
    return [
        (expert_index(x, z, c), expert_index(*move(x, z, c)))
        for x in range(EXPERTS)
        for z in range(Z)
        for c in range(CORES)
    ]


def turn(core):
    return 1 - 2 * core


def along_z(block, distance):
    route = expert_route(lambda x, z, c: (x, (z + distance * turn(c)) % Z, c))
    return lax.ppermute(block, "expert", route)


def along_x(block, distance):
    route = expert_route(lambda x, z, c: ((x + distance * turn(c)) % EXPERTS, z, c))
    return lax.ppermute(block, "expert", route)


def other_core(block):
    return lax.ppermute(block, "expert", expert_route(lambda x, z, c: (x, z, 1 - c)))


def to_section(block, step, distance):
    sections = lax.axis_size("pipe")
    width = EXPERTS * Z * CORES
    route = [
        (p * width + source, (p + step) * width + target)
        for p in range(sections)
        if 0 <= p + step < sections
        for source, target in expert_route(lambda x, z, c: (x, (z + distance * turn(c)) % Z, c))
    ]
    return lax.ppermute(block, ("pipe", "expert"), route)


def together(*values):
    return lax.optimization_barrier(values)


def expert_hot(routes):
    return routes[:, :, None] == jnp.arange(EXPERTS, dtype=jnp.int32)


def expert_shares(hot, gates):
    return jnp.sum(jnp.where(hot, gates[:, :, None], 0.0), axis=1)


def three_parts(values):
    first = lax.reduce_precision(values, 8, 7)
    second = lax.reduce_precision(values - first, 8, 7)
    return [part.astype(jnp.bfloat16) for part in (first, second, values - first - second)]


def side_columns(shares):
    parts = jnp.concatenate(three_parts(shares), axis=1)
    return jnp.pad(parts, ((0, 0), (0, LANES - parts.shape[1])))


def share_picks(experts):
    lane = jnp.arange(LANES, dtype=jnp.int32)
    wanted = jnp.stack(experts + [EXPERTS + e for e in experts])
    picks = (lane[:, None] % (2 * EXPERTS) == wanted[None, :]) & (lane[:, None] < 6 * EXPERTS)
    return jnp.pad(picks.astype(jnp.bfloat16), ((0, 0), (0, LANES - wanted.shape[0])))


def dot(a, b):
    return jnp.dot(a, b, preferred_element_type=jnp.float32)


def dot_t(a, b):
    return lax.dot_general(a, b, (((1,), (1,)), ((), ())), preferred_element_type=jnp.float32)


def join_kernel(gate_up, down, joined, done):
    model, depth = gate_up.shape[0], down.shape[0]
    piece = model // JOIN_PIECES
    pairs = [
        (gate_up.at[pl.ds(k * piece, piece), :], joined.at[pl.ds(k * piece, piece), :])
        for k in range(JOIN_PIECES)
    ]
    pairs += [
        (down.at[:, pl.ds(k * CHUNK, CHUNK)], joined.at[pl.ds(model + k * depth, depth), :])
        for k in range(model // CHUNK)
    ]
    copies = [
        pltpu.make_async_copy(source, target, done.at[k])
        for k, (source, target) in enumerate(pairs)
    ]
    for copy in copies:
        copy.start()
    for copy in copies:
        copy.wait()


def join_weights(gate_up, down):
    model, depth = gate_up.shape[0], down.shape[0]
    anywhere = pl.BlockSpec(memory_space=pl.ANY)
    rows = model + model // CHUNK * depth
    return pl.pallas_call(
        join_kernel,
        out_shape=jax.ShapeDtypeStruct((rows, CHUNK), gate_up.dtype),
        in_specs=[anywhere, anywhere],
        out_specs=pl.BlockSpec(memory_space=pltpu.VMEM),
        scratch_shapes=[pltpu.SemaphoreType.DMA((JOIN_PIECES + model // CHUNK,))],
    )(gate_up, down)


def fill_rows(mine, other, rows):
    half, model = mine.shape[0], rows[0].shape[1]
    for k, target in enumerate(rows):
        target[:half, :] = mine[:, k * model : (k + 1) * model]
        target[half:, :] = other[:, k * model : (k + 1) * model]


def pick_shares(mine, other, picks, model):
    sides = [part[:, 3 * model :] for part in (mine, other)]
    return jnp.concatenate([dot(side, picks[...]) for side in sides], axis=0)


def one_expert(rows, weight, share, back_share):
    token, saved, upstream = rows
    model, half = token.shape[1], CHUNK // 2
    cuts = [slice(low, low + CHUNK) for low in range(0, model, CHUNK)]
    downs = [slice(model + k * half, model + (k + 1) * half) for k in range(len(cuts))]
    gate_up = weight[:model, :]
    both = dot(token[...], gate_up)
    gate_val, up_val = both[:, :half], both[:, half:]
    hidden = (gate_val * jax.nn.sigmoid(gate_val) * up_val).astype(jnp.bfloat16)
    hidden_grad = sum(dot_t(upstream[:, cut], weight[at, :]) for cut, at in zip(cuts, downs))
    both = dot(saved[...], gate_up)
    gate_val, up_val = both[:, :half], both[:, half:]
    sig = jax.nn.sigmoid(gate_val)
    gate_grad = hidden_grad * up_val * sig * (1.0 + gate_val * (1.0 - sig))
    up_grad = hidden_grad * gate_val * sig
    grad = jnp.concatenate([gate_grad, up_grad], axis=1).astype(jnp.bfloat16)
    for cut, at in zip(cuts, downs):
        yield cut, share * dot(hidden, weight[at, :]), back_share * dot_t(grad, weight[cut, :])


def first_kernel(mine, other, picks, *refs):
    weights, (total, back_total), rows, shares = refs[:3], refs[3:5], refs[5:8], refs[8]
    fill_rows(mine, other, rows)
    shares[...] = pick_shares(mine, other, picks, rows[0].shape[1])
    for k, weight in enumerate(weights):
        share, back_share = shares[:, k : k + 1], shares[:, EXPERTS + k : EXPERTS + k + 1]
        for cut, out, back_out in one_expert(rows, weight, share, back_share):
            if k > 0:
                out, back_out = out + total[:, cut], back_out + back_total[:, cut]
            total[:, cut], back_total[:, cut] = out, back_out


def last_kernel(total, back_total, token, saved, upstream, shares, weight, keep, give):
    half, model = keep.shape[0], token.shape[1]
    share, back_share = shares[:, EXPERTS - 1 : EXPERTS], shares[:, 2 * EXPERTS - 1 : 2 * EXPERTS]
    for cut, out, back_out in one_expert((token, saved, upstream), weight, share, back_share):
        back_cut = slice(model + cut.start, model + cut.stop)
        out, back_out = out + total[:, cut], back_out + back_total[:, cut]
        keep[:, cut], keep[:, back_cut] = out[:half], back_out[:half]
        give[:, cut] = out[half:].astype(jnp.bfloat16)
        give[:, back_cut] = back_out[half:].astype(jnp.bfloat16)


def run_kernel(kernel, operands, outs):
    whole = pl.BlockSpec(memory_space=pltpu.VMEM)
    return pl.pallas_call(
        kernel,
        out_shape=outs,
        in_specs=[whole] * len(operands),
        out_specs=tuple(whole for _ in outs),
        compiler_params=pltpu.CompilerParams(vmem_limit_bytes=ROOM),
        cost_estimate=pl.CostEstimate(flops=1000, bytes_accessed=1000, transcendentals=0),
    )(*operands)


def on_device(
    forward_input,
    backward_input,
    backward_grad,
    gate_up_weight,
    down_weight,
    forward_routes,
    backward_routes,
    forward_gates,
    backward_gates,
):
    tokens, saved, upstream = forward_input[0], backward_input[0], backward_grad[0]
    rows, model = tokens.shape
    index = lax.axis_index("expert")
    turned = 1 - 2 * (index % CORES)
    me = index // (Z * CORES)
    experts = [(me + EXPERTS + d * turned) % EXPERTS for d in (0, -1, 1, -2)]

    with jax.named_scope("gather_weights"):
        weights = join_weights(gate_up_weight[0], down_weight[0])
        near, far = along_x(weights, 1), along_x(weights, -1)
    with jax.named_scope("gather_rows"):
        shares = [
            expert_shares(expert_hot(forward_routes[0]), forward_gates[0]),
            expert_shares(expert_hot(backward_routes[0]), backward_gates[0]),
        ]
        side = side_columns(jnp.concatenate(shares, axis=1))
        mine = jnp.concatenate([tokens, saved, upstream, side], axis=1)
        below, above = along_z(mine, 1), along_z(mine, -1)
        opposite = along_z(below, 1)
    with jax.named_scope("gather_opposite"):
        near, far, below, above, opposite = together(near, far, below, above, opposite)
        weights = [weights, near, far, along_x(near, 1)]
        mine = jnp.concatenate([mine, below, above, opposite], axis=0)
        other = other_core(mine)
    half = Z * rows
    with jax.named_scope("experts"):
        outs = [jax.ShapeDtypeStruct((2 * half, model), jnp.float32)] * 2
        outs += [jax.ShapeDtypeStruct((2 * half, model), jnp.bfloat16)] * 3
        outs += [jax.ShapeDtypeStruct((2 * half, LANES), jnp.float32)]
        sums = run_kernel(first_kernel, (mine, other, share_picks(experts), *weights[:3]), outs)
    with jax.named_scope("residual"):
        tokens, upstream, *sums = together(tokens, upstream, *sums)
        residuals = to_section(tokens, 1, 0), to_section(upstream, -1, 0)
        *residuals, last_weight = together(*residuals, weights[3])
    with jax.named_scope("last_expert"):
        outs = (
            jax.ShapeDtypeStruct((half, 2 * model), jnp.float32),
            jax.ShapeDtypeStruct((half, 2 * model), jnp.bfloat16),
        )
        keep, give = run_kernel(last_kernel, (*sums, last_weight), outs)
    with jax.named_scope("cores"):
        total = keep + other_core(give).astype(jnp.float32)
    with jax.named_scope("home"):
        own, near, far, passed = jnp.split(total, Z, axis=0)
        passed = along_z(passed.astype(jnp.bfloat16), -1)
        own, far = own.astype(jnp.bfloat16), far.astype(jnp.bfloat16)
        parts = [to_section(far[:, :model], 1, 1), to_section(far[:, model:], -1, 1)]
        passed, *parts = together(passed, *parts)
        near = (near + passed.astype(jnp.float32)).astype(jnp.bfloat16)
        parts += [to_section(near[:, :model], 1, -1), to_section(near[:, model:], -1, -1)]
        parts += [to_section(own[:, :model], 1, 0), to_section(own[:, model:], -1, 0)]
        sides = [[residuals[k]] + parts[k::2] for k in range(2)]
        forward_next, backward_next = [
            sum(part.astype(jnp.float32) for part in side).astype(jnp.bfloat16) for side in sides
        ]
    return (forward_next[None], backward_next[None])


def solution(mesh):
    by_token = P("pipe", "expert", None)
    return jax.shard_map(
        on_device,
        mesh=mesh,
        in_specs=(by_token,) * 3 + (P("pipe", None, "expert"),) + (by_token,) * 5,
        out_specs=(by_token, by_token),
        check_vma=False,
    )
```

```python
import jax
import jax.numpy as jnp
from jax import lax
from jax.experimental import pallas as pl
from jax.experimental.pallas import tpu as pltpu
from jax.sharding import PartitionSpec as P

EXPERTS = 4
Z = 4
CORES = 2
LANES = 128
CHUNK = 256
JOIN_PIECES = 4
ROOM = 40 * 1024 * 1024


def expert_index(x, z, core):
    return (x * Z + z) * CORES + core


def expert_route(move):
    return [
        (expert_index(x, z, c), expert_index(*move(x, z, c)))
        for x in range(EXPERTS)
        for z in range(Z)
        for c in range(CORES)
    ]


def turn(core):
    return 1 - 2 * core


def along_z(block, distance):
    route = expert_route(lambda x, z, c: (x, (z + distance * turn(c)) % Z, c))
    return lax.ppermute(block, "expert", route)


def along_x(block, distance):
    route = expert_route(lambda x, z, c: ((x + distance * turn(c)) % EXPERTS, z, c))
    return lax.ppermute(block, "expert", route)


def other_core(block):
    return lax.ppermute(block, "expert", expert_route(lambda x, z, c: (x, z, 1 - c)))


def to_section(block, step, distance):
    sections = lax.axis_size("pipe")
    width = EXPERTS * Z * CORES
    route = [
        (p * width + source, (p + step) * width + target)
        for p in range(sections)
        if 0 <= p + step < sections
        for source, target in expert_route(lambda x, z, c: (x, (z + distance * turn(c)) % Z, c))
    ]
    return lax.ppermute(block, ("pipe", "expert"), route)


def together(*values):
    return lax.optimization_barrier(values)


def expert_hot(routes):
    return routes[:, :, None] == jnp.arange(EXPERTS, dtype=jnp.int32)


def expert_shares(hot, gates):
    return jnp.sum(jnp.where(hot, gates[:, :, None], 0.0), axis=1)


def three_parts(values):
    first = lax.reduce_precision(values, 8, 7)
    second = lax.reduce_precision(values - first, 8, 7)
    return [part.astype(jnp.bfloat16) for part in (first, second, values - first - second)]


def side_columns(shares):
    parts = jnp.concatenate(three_parts(shares), axis=1)
    return jnp.pad(parts, ((0, 0), (0, LANES - parts.shape[1])))


def share_picks(experts):
    lane = jnp.arange(LANES, dtype=jnp.int32)
    wanted = jnp.stack(experts + [EXPERTS + e for e in experts])
    picks = (lane[:, None] % (2 * EXPERTS) == wanted[None, :]) & (lane[:, None] < 6 * EXPERTS)
    return jnp.pad(picks.astype(jnp.bfloat16), ((0, 0), (0, LANES - wanted.shape[0])))


def dot(a, b):
    return jnp.dot(a, b, preferred_element_type=jnp.float32)


def dot_t(a, b):
    return lax.dot_general(a, b, (((1,), (1,)), ((), ())), preferred_element_type=jnp.float32)


def join_kernel(gate_up, down, joined, done):
    model, depth = gate_up.shape[0], down.shape[0]
    piece = model // JOIN_PIECES
    pairs = [
        (gate_up.at[pl.ds(k * piece, piece), :], joined.at[pl.ds(k * piece, piece), :])
        for k in range(JOIN_PIECES)
    ]
    pairs += [
        (down.at[:, pl.ds(k * CHUNK, CHUNK)], joined.at[pl.ds(model + k * depth, depth), :])
        for k in range(model // CHUNK)
    ]
    copies = [
        pltpu.make_async_copy(source, target, done.at[k])
        for k, (source, target) in enumerate(pairs)
    ]
    for copy in copies:
        copy.start()
    for copy in copies:
        copy.wait()


def join_weights(gate_up, down):
    model, depth = gate_up.shape[0], down.shape[0]
    anywhere = pl.BlockSpec(memory_space=pl.ANY)
    rows = model + model // CHUNK * depth
    return pl.pallas_call(
        join_kernel,
        out_shape=jax.ShapeDtypeStruct((rows, CHUNK), gate_up.dtype),
        in_specs=[anywhere, anywhere],
        out_specs=pl.BlockSpec(memory_space=pltpu.VMEM),
        scratch_shapes=[pltpu.SemaphoreType.DMA((JOIN_PIECES + model // CHUNK,))],
    )(gate_up, down)


def fill_rows(mine, other, rows):
    half, model = mine.shape[0], rows[0].shape[1]
    for k, target in enumerate(rows):
        target[:half, :] = mine[:, k * model : (k + 1) * model]
        target[half:, :] = other[:, k * model : (k + 1) * model]


def pick_shares(mine, other, picks, model):
    sides = [part[:, 3 * model :] for part in (mine, other)]
    return jnp.concatenate([dot(side, picks[...]) for side in sides], axis=0)


def one_expert(rows, weight, share, back_share):
    token, saved, upstream = rows
    model, half = token.shape[1], CHUNK // 2
    cuts = [slice(low, low + CHUNK) for low in range(0, model, CHUNK)]
    downs = [slice(model + k * half, model + (k + 1) * half) for k in range(len(cuts))]
    gate_up = weight[:model, :]
    both = dot(token[...], gate_up)
    gate_val, up_val = both[:, :half], both[:, half:]
    hidden = (gate_val * jax.nn.sigmoid(gate_val) * up_val).astype(jnp.bfloat16)
    hidden_grad = sum(dot_t(upstream[:, cut], weight[at, :]) for cut, at in zip(cuts, downs))
    both = dot(saved[...], gate_up)
    gate_val, up_val = both[:, :half], both[:, half:]
    sig = jax.nn.sigmoid(gate_val)
    gate_grad = hidden_grad * up_val * sig * (1.0 + gate_val * (1.0 - sig))
    up_grad = hidden_grad * gate_val * sig
    grad = jnp.concatenate([gate_grad, up_grad], axis=1).astype(jnp.bfloat16)
    for cut, at in zip(cuts, downs):
        yield cut, share * dot(hidden, weight[at, :]), back_share * dot_t(grad, weight[cut, :])


def first_kernel(mine, other, picks, *refs):
    weights, (total, back_total), rows, shares = refs[:3], refs[3:5], refs[5:8], refs[8]
    fill_rows(mine, other, rows)
    shares[...] = pick_shares(mine, other, picks, rows[0].shape[1])
    for k, weight in enumerate(weights):
        share, back_share = shares[:, k : k + 1], shares[:, EXPERTS + k : EXPERTS + k + 1]
        for cut, out, back_out in one_expert(rows, weight, share, back_share):
            if k > 0:
                out, back_out = out + total[:, cut], back_out + back_total[:, cut]
            total[:, cut], back_total[:, cut] = out, back_out


def last_kernel(total, back_total, token, saved, upstream, shares, weight, keep, give):
    half, model = keep.shape[0], token.shape[1]
    share, back_share = shares[:, EXPERTS - 1 : EXPERTS], shares[:, 2 * EXPERTS - 1 : 2 * EXPERTS]
    for cut, out, back_out in one_expert((token, saved, upstream), weight, share, back_share):
        back_cut = slice(model + cut.start, model + cut.stop)
        out, back_out = out + total[:, cut], back_out + back_total[:, cut]
        keep[:, cut], keep[:, back_cut] = out[:half], back_out[:half]
        give[:, cut] = out[half:].astype(jnp.bfloat16)
        give[:, back_cut] = back_out[half:].astype(jnp.bfloat16)


def run_kernel(kernel, operands, outs):
    whole = pl.BlockSpec(memory_space=pltpu.VMEM)
    return pl.pallas_call(
        kernel,
        out_shape=outs,
        in_specs=[whole] * len(operands),
        out_specs=tuple(whole for _ in outs),
        compiler_params=pltpu.CompilerParams(vmem_limit_bytes=ROOM),
        cost_estimate=pl.CostEstimate(flops=1000, bytes_accessed=1000, transcendentals=0),
    )(*operands)


def on_device(
    forward_input,
    backward_input,
    backward_grad,
    gate_up_weight,
    down_weight,
    forward_routes,
    backward_routes,
    forward_gates,
    backward_gates,
):
    tokens, saved, upstream = forward_input[0], backward_input[0], backward_grad[0]
    rows, model = tokens.shape
    index = lax.axis_index("expert")
    turned = 1 - 2 * (index % CORES)
    me = index // (Z * CORES)
    experts = [(me + EXPERTS + d * turned) % EXPERTS for d in (0, -1, 1, -2)]

    with jax.named_scope("gather_weights"):
        weights = join_weights(gate_up_weight[0], down_weight[0])
        near, far = along_x(weights, 1), along_x(weights, -1)
    with jax.named_scope("gather_rows"):
        shares = [
            expert_shares(expert_hot(forward_routes[0]), forward_gates[0]),
            expert_shares(expert_hot(backward_routes[0]), backward_gates[0]),
        ]
        side = side_columns(jnp.concatenate(shares, axis=1))
        mine = jnp.concatenate([tokens, saved, upstream, side], axis=1)
        below, above = along_z(mine, 1), along_z(mine, -1)
        opposite = along_z(below, 1)
    with jax.named_scope("gather_opposite"):
        near, far, below, above, opposite = together(near, far, below, above, opposite)
        weights = [weights, near, far, along_x(near, 1)]
        mine = jnp.concatenate([mine, below, above, opposite], axis=0)
        other = other_core(mine)
    half = Z * rows
    with jax.named_scope("experts"):
        outs = [jax.ShapeDtypeStruct((2 * half, model), jnp.float32)] * 2
        outs += [jax.ShapeDtypeStruct((2 * half, model), jnp.bfloat16)] * 3
        outs += [jax.ShapeDtypeStruct((2 * half, LANES), jnp.float32)]
        sums = run_kernel(first_kernel, (mine, other, share_picks(experts), *weights[:3]), outs)
    with jax.named_scope("residual"):
        tokens, upstream, *sums = together(tokens, upstream, *sums)
        residuals = to_section(tokens, 1, 0), to_section(upstream, -1, 0)
        *residuals, last_weight = together(*residuals, weights[3])
    with jax.named_scope("last_expert"):
        outs = (
            jax.ShapeDtypeStruct((half, 2 * model), jnp.float32),
            jax.ShapeDtypeStruct((half, 2 * model), jnp.bfloat16),
        )
        keep, give = run_kernel(last_kernel, (*sums, last_weight), outs)
    with jax.named_scope("cores"):
        total = keep + other_core(give).astype(jnp.float32)
    with jax.named_scope("home"):
        own, near, far, passed = jnp.split(total, Z, axis=0)
        passed = along_z(passed.astype(jnp.bfloat16), -1)
        own, far = own.astype(jnp.bfloat16), far.astype(jnp.bfloat16)
        parts = [to_section(far[:, :model], 1, 1), to_section(far[:, model:], -1, 1)]
        parts += [to_section(own[:, :model], 1, 0), to_section(own[:, model:], -1, 0)]
        passed, *parts = together(passed, *parts)
        near = (near + passed.astype(jnp.float32)).astype(jnp.bfloat16)
        parts += [to_section(near[:, :model], 1, -1), to_section(near[:, model:], -1, -1)]
        sides = [[residuals[k]] + parts[k::2] for k in range(2)]
        forward_next, backward_next = [
            sum(part.astype(jnp.float32) for part in side).astype(jnp.bfloat16) for side in sides
        ]
    return (forward_next[None], backward_next[None])


def solution(mesh):
    by_token = P("pipe", "expert", None)
    return jax.shard_map(
        on_device,
        mesh=mesh,
        in_specs=(by_token,) * 3 + (P("pipe", None, "expert"),) + (by_token,) * 5,
        out_specs=(by_token, by_token),
        check_vma=False,
    )
```
